256 devices in a mesh: boot: 8 (over z), tm: 32 (over x, y, core).
Axes of the slice: x: 4, y: 4, z: 8, core: 2. Of those that a mesh axis runs over, the one named last changes fastest.
Arguments:
- recording: bfloat16 [16384, 1024], P('tm'), may hold values from -60 to 60, as said below
- starts: int32 [8, 192], P('boot', 'tm'), may hold values from 0 to 448, as said below
- lengths: int32 [8, 192], P('boot', 'tm'), may hold values from 1 to 64, as said below
- support: int32 [8, 4096], P(None, 'boot'), may hold values 0 or 1
Outputs:
- averaged: float32 [32, 4096], P(None, 'boot')
- residual: float32 [32, 16384], P(None, 'tm')
The draws below stay inside these ranges and needn't reach their ends.
Inputs may be any that keep to these rules, and one draw needn't show every extreme that they name: A shard's values are an autoregressive recording; its values stay within the range. Entry [b, j * 6 + k] starts block k of resample b on time shard j, counted from the shard's first sample; a block ends inside its shard. The 6 lengths of one resample on one time shard sum to at most 384.
All inputs are finite; a program needn't handle non-finite values. No bound on the sum of `support` on one device may be relied on, other than what follows from the above.
Results may differ from the reference program's by a relative error of at most 0.0043.
The reference program's roundings to bfloat16 on the way count: a program that leaves them out, or rounds other values in their place, can miss the bound.
Values may be sent and summed in bfloat16 or wider, within the bound.
A program may use at most 64 MiB of HBM per device.

```python
import jax
import jax.numpy as jnp
from jax import lax

CHANNEL_COUNT = 1024
LAGS = 4
FEAT = 4096
RESPONSE_COUNT = 32
BOOTS = 8
SEG = 512
NBLK = 6
MOST_LEN = 64
CAP = 384
ITERS = 3
CHEB = 5
SAMPLE_COUNT = 16384
N_TM = 32


def draw_recording(key, part):
    first, second = jax.random.split(jax.random.fold_in(key, 5), 2)
    rate = jnp.exp(jax.random.uniform(first, (CHANNEL_COUNT,), jnp.float32, jnp.log(0.3), jnp.log(0.95)))
    noise = jax.random.normal(second, (SAMPLE_COUNT, CHANNEL_COUNT), jnp.float32)
    keeps = jnp.sqrt(1.0 - rate * rate)

    def advance(before, fresh):
        after = rate * before + keeps * fresh
        return (after, after)
    unused, later = lax.scan(advance, noise[0], noise[1:])
    series = jnp.concatenate([noise[:1], later], axis=0)
    envelope = 1.0 + 2.0 * jnp.arange(SAMPLE_COUNT, dtype=jnp.float32) / max(SAMPLE_COUNT - 1, 1)
    series = series * envelope[:, None]
    return jnp.clip(series, -60.0, 60.0).astype(jnp.bfloat16)


def block_plan(key):
    first, second, third, fourth = jax.random.split(jax.random.fold_in(key, 11), 4)
    ceiling = jax.random.randint(first, (BOOTS, N_TM, 1), MOST_LEN // 4, MOST_LEN + 1)
    raw = jax.random.randint(second, (BOOTS, N_TM, NBLK), 0, 1 << 20)
    sizes = 1 + raw % ceiling
    full_shard = jax.random.randint(third, (BOOTS,), 0, N_TM)
    forced = (jnp.arange(N_TM)[None, :] == full_shard[:, None])[:, :, None]
    sizes = jnp.where(forced, MOST_LEN, sizes)
    begins = jax.random.randint(fourth, (BOOTS, N_TM, NBLK), 0, SEG - MOST_LEN + 1)
    blocks = jnp.arange(NBLK)[None, None, :]
    begins = jnp.where(forced & (blocks == 0), SEG - MOST_LEN, begins)
    begins = jnp.where(forced & (blocks == 1), 0, begins)
    return (begins.reshape(BOOTS, N_TM * NBLK).astype(jnp.int32), sizes.reshape(BOOTS, N_TM * NBLK).astype(jnp.int32))


def draw_starts(key, part):
    return block_plan(key)[0]


def draw_lengths(key, part):
    return block_plan(key)[1]


def place_ends(values, own_key, least, largest):
    longest = values.shape.index(max(values.shape))
    spots = []
    for shift in (0, 1):
        where = [jax.random.randint(jax.random.fold_in(own_key, axis), (), 0, length) for axis, length in enumerate(values.shape)]
        where[longest] = (where[longest] + shift) % values.shape[longest]
        spots.append(tuple(where))
    return values.at[spots[0]].set(least).at[spots[1]].set(largest)


def setup_inputs(seed: int = 0) -> dict:
    arg_keys = jax.random.split(jax.random.key(seed), 5)
    return {
        "recording": draw_recording(jax.random.fold_in(arg_keys[4], 71), 0),
        "starts": draw_starts(jax.random.fold_in(arg_keys[4], 71), 0),
        "lengths": draw_lengths(jax.random.fold_in(arg_keys[4], 71), 0),
        "support": place_ends((jax.random.randint(arg_keys[3], (BOOTS, FEAT), 0, 4) < 1).astype(jnp.int32), jax.random.fold_in(arg_keys[3], 1), 0, 1),
    }


ridge_weight = 4.0
shrink_level = 0.75
epsilon = 1e-05

def bootstrap_rows(window, begins, sizes):
    ends = jnp.cumsum(sizes)
    offsets = ends - sizes
    total = ends[-1]
    rows = jnp.arange(CAP, dtype=jnp.int32)
    member = (rows[:, None] >= offsets[None, :]).astype(jnp.int32)
    which = lax.optimization_barrier(jnp.sum(member, axis=1)) - 1
    picked = (which[:, None] == jnp.arange(NBLK, dtype=jnp.int32)[None, :]).astype(jnp.int32)
    anchor = lax.optimization_barrier(jnp.sum(picked * offsets[None, :], axis=1))
    opening = lax.optimization_barrier(jnp.sum(picked * begins[None, :], axis=1))
    live = rows < total
    times = jnp.where(live, opening + rows - anchor, 0).astype(jnp.int32)
    blocks = [jnp.take(window, times + LAGS - 1 - delay_step, axis=0) for delay_step in range(LAGS)]
    design = jnp.concatenate(blocks, axis=1)
    design = jnp.where(live[:, None], design, jnp.zeros_like(design))
    answer = jnp.take(window[:, :RESPONSE_COUNT], times + LAGS, axis=0)
    answer = jnp.where(live[:, None], answer, jnp.zeros_like(answer))
    return (design, answer.T)

def chebyshev(gram, rhs, bound):
    center = ridge_weight + 0.5 * bound
    radius = 0.5 * bound
    sigma = center / radius
    solution = jnp.zeros_like(rhs)
    remain = rhs
    factor = 1.0 / sigma
    update = rhs / center
    for count in range(CHEB):
        solution = solution + update
        if count + 1 < CHEB:
            applied = ridge_weight * update + jnp.dot(update, gram, precision=lax.Precision.HIGHEST)
            remain = remain - applied
            after = 1.0 / (2.0 * sigma - factor)
            update = after * factor * update + 2.0 * after / radius * remain
            factor = after
    return solution

def prepare(design, answer):
    row_scale = 1.0 / CAP
    cross = jnp.dot(answer, design, preferred_element_type=jnp.float32) * row_scale
    gram = jnp.dot(design, design.T, preferred_element_type=jnp.float32) * row_scale
    bound = jnp.sqrt(jnp.sum(gram * gram))
    return (cross, gram, bound)

def local_solve(design, cross, gram, bound, consensus, dual):
    row_scale = 1.0 / CAP
    target = cross + ridge_weight * (consensus - dual)
    projected = lax.dot_general(target.astype(jnp.bfloat16), design, (((1,), (1,)), ((), ())), preferred_element_type=jnp.float32) * row_scale
    weights = chebyshev(gram, projected, bound)
    back = jnp.dot(weights.astype(jnp.bfloat16), design, preferred_element_type=jnp.float32)
    return (target - back) / ridge_weight

def shrink(mean_value):
    norms = jnp.sqrt(lax.optimization_barrier(jnp.sum(mean_value * mean_value, axis=0)))
    level = shrink_level * jnp.mean(norms)
    return mean_value * (jnp.maximum(norms - level, 0.0) / jnp.maximum(norms, level))[None, :]

def reference(recording, starts, lengths, support):
    values = recording.astype(jnp.float32)
    power = lax.optimization_barrier(jnp.sum(values * values, axis=0))
    scale = 1.0 / jnp.sqrt(power / SAMPLE_COUNT + epsilon)
    scaled_input = (values * scale).astype(jnp.bfloat16)
    extended = jnp.concatenate([jnp.zeros((LAGS, CHANNEL_COUNT), jnp.bfloat16), scaled_input], axis=0)
    shard_ids = jnp.arange(N_TM, dtype=jnp.int32)

    def window_of(shard):
        return lax.dynamic_slice_in_dim(extended, (shard * SEG).astype(jnp.int32), SEG + LAGS, 0)

    def fit_boot(plan):
        begins = plan[0].reshape(N_TM, NBLK)
        sizes = plan[1].reshape(N_TM, NBLK)
        windows = jax.vmap(window_of)(shard_ids)
        design, answer = jax.vmap(bootstrap_rows)(windows, begins, sizes)
        cross, gram, bound = jax.vmap(prepare)(design, answer)
        consensus = jnp.zeros((RESPONSE_COUNT, LAGS * CHANNEL_COUNT), jnp.float32)
        dual = jnp.zeros_like(cross)
        for rounds in range(ITERS):
            local = jax.vmap(local_solve, in_axes=(0, 0, 0, 0, None, 0))(design, cross, gram, bound, consensus, dual)
            mean_value = lax.optimization_barrier(jnp.sum(local + dual, axis=0)) / N_TM
            consensus = shrink(mean_value)
            dual = dual + local - consensus[None]
        return consensus
    estimates = lax.map(fit_boot, (starts, lengths))
    chosen = support.astype(jnp.float32)
    tally = lax.optimization_barrier(jnp.sum(chosen, axis=0))
    averaged = lax.optimization_barrier(jnp.sum(chosen[:, None, :] * estimates, axis=0)) / jnp.maximum(tally, 1.0)[None, :]
    lowered_program = averaged.astype(jnp.bfloat16)
    predicted_output = jnp.zeros((RESPONSE_COUNT, SAMPLE_COUNT), jnp.float32)
    for delay_step in range(LAGS):
        source_program = extended[LAGS - 1 - delay_step:LAGS - 1 - delay_step + SAMPLE_COUNT]
        predicted_output = predicted_output + lax.dot_general(lowered_program[:, delay_step * CHANNEL_COUNT:(delay_step + 1) * CHANNEL_COUNT], source_program, (((1,), (1,)), ((), ())), preferred_element_type=jnp.float32)
    residual = scaled_input[:, :RESPONSE_COUNT].astype(jnp.float32).T - predicted_output
    return (averaged, residual)
```

```python
import functools

import jax
import jax.numpy as jnp
from jax import lax
from jax.experimental import pallas as pl
from jax.experimental.pallas import tpu as pltpu
from jax.sharding import PartitionSpec as P

CHANNELS = 1024
LAGS = 4
FEAT = LAGS * CHANNELS
RESP = 32
NBLK = 6
CAP = 384
SEG = 512
ITERS = 3
CHEB = 5
HEAD = 16
WINDOW = 640
CHUNK = 128

RHO = 4.0
SHRINK = 0.75
EPSILON = 1e-05

HIGHEST = lax.Precision.HIGHEST
NT = (((1,), (1,)), ((), ()))
HALO, POWER, SUPPORT, SCATTER, GATHER, NORMS, BOOTS, FINAL = 0, 1, 2, 3, 6, 8, 9, 10
PHASES = 11


def chebyshev_terms(bound):
    theta = RHO + 0.5 * bound
    delta = 0.5 * bound
    sigma = theta / delta
    nought = jnp.zeros_like(bound)
    total = [nought] * CHEB
    remain = [jnp.ones_like(bound)] + [nought] * (CHEB - 1)
    factor = 1.0 / sigma
    update = [term / theta for term in remain]
    for count in range(CHEB):
        total = [a + b for a, b in zip(total, update)]
        if count + 1 < CHEB:
            applied = [
                theta * update[k] + (delta * update[k - 1] if k else 0.0)
                for k in range(CHEB)
            ]
            remain = [a - b for a, b in zip(remain, applied)]
            after = 1.0 / (2.0 * sigma - factor)
            update = [
                after * factor * d + 2.0 * after / delta * r
                for d, r in zip(update, remain)
            ]
            factor = after
    return total, delta


def kernel(
    tm,
    boots,
    rec_ref,
    starts_ref,
    lengths_ref,
    support_ref,
    avg_ref,
    res_ref,
    halo,
    power,
    sup,
    ext,
    design,
    cross,
    v,
    z,
    tb,
    outgoing,
    incoming,
    gathered,
    norms,
    zx,
    final,
    send_sem,
    recv_sem,
):
    b = lax.axis_index("boot")
    me = lax.axis_index("tm")

    def tm_peer(i):
        return lax.rem(me + i, tm)

    def boot_peer(i):
        return lax.rem(b + i, boots)

    barrier = pltpu.get_barrier_semaphore()

    @pl.loop(1, tm)
    def _(i):
        pl.semaphore_signal(
            barrier, inc=1, device_id={"tm": tm_peer(i)}, device_id_type=pl.DeviceIdType.MESH
        )

    @pl.loop(1, boots)
    def _(i):
        pl.semaphore_signal(
            barrier, inc=1, device_id={"boot": boot_peer(i)}, device_id_type=pl.DeviceIdType.MESH
        )

    def send(src, dst, phase, target):
        pltpu.make_async_remote_copy(
            src_ref=src,
            dst_ref=dst,
            send_sem=send_sem.at[phase],
            recv_sem=recv_sem.at[phase],
            device_id=target,
            device_id_type=pl.DeviceIdType.MESH,
        ).start()

    def to_tm(src, dst, phase):
        @pl.loop(1, tm)
        def _(i):
            send(src, dst, phase, {"tm": tm_peer(i)})

    def to_boots(src, dst, phase):
        @pl.loop(1, boots)
        def _(i):
            send(src, dst, phase, {"boot": boot_peer(i)})

    def arrived(ref, phase):
        pltpu.make_async_copy(ref, ref, recv_sem.at[phase]).wait()

    def left(ref, phase):
        pltpu.make_async_copy(ref, ref, send_sem.at[phase]).wait()

    acc = jnp.zeros((8, CHANNELS), jnp.float32)

    def add_rows(k, acc):
        block = rec_ref[pl.ds(pl.multiple_of(k * 16, 16), 16), :].astype(jnp.float32)
        block = block * block
        return acc + block[:8] + block[8:]

    acc = lax.fori_loop(0, SEG // 16, add_rows, acc)
    power[me] = jnp.sum(acc, axis=0, keepdims=True)

    pl.semaphore_wait(barrier, tm + boots - 2)
    to_tm(power.at[me], power.at[me], POWER)
    send(rec_ref.at[pl.ds(SEG - HEAD, HEAD)], halo, HALO, {"tm": tm_peer(1)})
    to_boots(support_ref, sup.at[b], SUPPORT)
    sup[b] = support_ref[...]

    row = lax.broadcasted_iota(jnp.int32, (CAP, CHUNK), 0)
    place = jnp.full((CAP, CHUNK), -4 * WINDOW, jnp.int32)
    offset = jnp.int32(0)
    for k in range(NBLK):
        length = lengths_ref[0, k]
        inside = (row >= offset) & (row < offset + length)
        place = jnp.where(inside, row + (starts_ref[0, k] - offset + HEAD), place)
        offset = offset + length
    lane = lax.broadcasted_iota(jnp.int32, (CAP, CHUNK), 1)

    def picks(back):
        return jnp.concatenate(
            [
                jnp.where(place - back == lane + c * CHUNK, 1.0, 0.0).astype(jnp.bfloat16)
                for c in range(WINDOW // CHUNK)
            ],
            axis=1,
        )

    arrived(power.at[pl.ds(0, tm - 1)], POWER)
    total = jnp.sum(power[...], axis=0)
    scale = 1.0 / jnp.sqrt(total / (SEG * tm) + EPSILON)

    def scale_rows(k, carry):
        at = pl.multiple_of(k * 16, 16)
        block = rec_ref[pl.ds(at, 16), :].astype(jnp.float32) * scale
        ext[pl.ds(pl.multiple_of(at + HEAD, 16), 16), :] = block.astype(jnp.bfloat16)
        return carry

    lax.fori_loop(0, SEG // 16, scale_rows, 0)
    arrived(halo, HALO)
    first = (halo[...].astype(jnp.float32) * scale).astype(jnp.bfloat16)
    ext[0:HEAD, :] = jnp.where(me == 0, jnp.zeros_like(first), first)
    ext[HEAD + SEG :, :] = jnp.zeros((WINDOW - HEAD - SEG, CHANNELS), jnp.bfloat16)

    answer = jnp.dot(picks(0), ext[:, :CHUNK], preferred_element_type=jnp.float32)
    answer = jnp.transpose(answer)[:RESP].astype(jnp.bfloat16)
    gram = jnp.zeros((CAP, CAP), jnp.float32)
    for lag in range(LAGS):
        pick = picks(1 + lag)
        for part in range(4):
            at = lag * CHANNELS + part * 256
            block = jnp.dot(
                pick, ext[:, part * 256 : (part + 1) * 256], preferred_element_type=jnp.float32
            ).astype(jnp.bfloat16)
            design[:, at : at + 256] = block
            fit = jnp.dot(answer, block, preferred_element_type=jnp.float32) * (1.0 / CAP)
            cross[:, at : at + 256] = fit
            tb[:, at : at + 256] = fit.astype(jnp.bfloat16)
        piece = design[:, lag * CHANNELS : (lag + 1) * CHANNELS]
        gram = gram + lax.dot_general(piece, piece, NT, preferred_element_type=jnp.float32)
    gram = gram * (1.0 / CAP)
    bound = jnp.sqrt(jnp.sum(jnp.sum(gram * gram, axis=1, keepdims=True), axis=0, keepdims=True))
    terms, delta = chebyshev_terms(bound)
    ri = lax.broadcasted_iota(jnp.int32, (CAP, CAP), 0)
    ci = lax.broadcasted_iota(jnp.int32, (CAP, CAP), 1)
    eye = jnp.where(ri == ci, 1.0, 0.0)
    x1 = gram * (1.0 / delta) - eye
    x2 = jnp.dot(x1, x1, precision=HIGHEST, preferred_element_type=jnp.float32)
    solver = (
        terms[0] * eye
        + terms[1] * x1
        + terms[2] * x2
        + jnp.dot(
            x2, terms[3] * x1 + terms[4] * x2, precision=HIGHEST, preferred_element_type=jnp.float32
        )
    )

    mine = pl.ds(pl.multiple_of(me * CHUNK, CHUNK), CHUNK)
    for it in range(ITERS):
        projected = jnp.zeros((RESP, CAP), jnp.float32)
        for part in range(8):
            cols = slice(part * 512, (part + 1) * 512)
            projected = projected + lax.dot_general(
                tb[:, cols], design[:, cols], NT, preferred_element_type=jnp.float32
            )
        projected = projected * (1.0 / CAP)
        weights = jnp.dot(
            projected, solver, precision=HIGHEST, preferred_element_type=jnp.float32
        ).astype(jnp.bfloat16)
        if it:
            left(outgoing.at[pl.ds(0, tm - 1)], SCATTER + it - 1)
        for part in range(8):
            cols = slice(part * 512, (part + 1) * 512)
            back = jnp.dot(weights, design[:, cols], preferred_element_type=jnp.float32)
            value = (cross[:, cols] - back) * (1.0 / RHO)
            v[:, cols] = value
            for c in range(4):
                outgoing[part * 4 + c] = value[:, c * CHUNK : (c + 1) * CHUNK].astype(jnp.bfloat16)

        @pl.loop(1, tm)
        def _(i):
            peer = tm_peer(i)
            send(outgoing.at[peer], incoming.at[i - 1], SCATTER + it, {"tm": peer})

        arrived(incoming, SCATTER + it)
        mean = v[:, mine]
        for i in range(tm - 1):
            mean = mean + incoming[i].astype(jnp.float32)
        mean = mean * (1.0 / tm)
        if it:
            mean = mean + z[:, mine]
        if it + 1 < ITERS:
            if it:
                left(gathered.at[pl.ds(0, tm - 1)], GATHER + it - 1)
            gathered[me] = mean.astype(jnp.bfloat16)
            to_tm(gathered.at[me], gathered.at[me], GATHER + it)
            arrived(gathered.at[pl.ds(0, tm - 1)], GATHER + it)
            lengths = []
            for c in range(tm):
                block = gathered[c].astype(jnp.float32)
                lengths.append(jnp.sqrt(jnp.sum(block * block, axis=0, keepdims=True)))
            level = (
                jnp.sum(functools.reduce(jnp.add, lengths), axis=1, keepdims=True)
                * (SHRINK / FEAT)
            )
            for c in range(tm):
                cols = slice(c * CHUNK, (c + 1) * CHUNK)
                factor = jnp.maximum(lengths[c] - level, 0.0) / jnp.maximum(lengths[c], level)
                fresh = gathered[c].astype(jnp.float32) * factor
                dual = v[:, cols] - fresh
                if it:
                    dual = dual + z[:, cols]
                z[:, cols] = fresh
                tb[:, cols] = (cross[:, cols] + RHO * (fresh - dual)).astype(jnp.bfloat16)

    length = jnp.sqrt(jnp.sum(mean * mean, axis=0, keepdims=True))
    norms[me] = length
    to_tm(norms.at[me], norms.at[me], NORMS)
    arrived(norms.at[pl.ds(0, tm - 1)], NORMS)
    level = jnp.sum(jnp.sum(norms[...], axis=0), axis=1, keepdims=True) * (SHRINK / FEAT)
    factor = jnp.maximum(length - level, 0.0) / jnp.maximum(length, level)
    zx[b] = (mean * factor).astype(jnp.bfloat16)
    to_boots(zx.at[b], zx.at[b], BOOTS)
    arrived(sup.at[pl.ds(0, boots - 1)], SUPPORT)
    quarter = pl.ds(pl.multiple_of(lax.rem(me, 4) * CHUNK, CHUNK), CHUNK)
    chosen = sup[me // 4, :, quarter].astype(jnp.float32)
    tally = jnp.maximum(jnp.sum(chosen, axis=0, keepdims=True), 1.0)
    arrived(zx.at[pl.ds(0, boots - 1)], BOOTS)
    average = jnp.zeros((RESP, CHUNK), jnp.float32)
    for k in range(boots):
        average = average + chosen[k : k + 1] * zx[k].astype(jnp.float32)
    average = average / tally
    final[me] = average.astype(jnp.bfloat16)
    to_tm(final.at[me], final.at[me], FINAL)
    normed = jnp.transpose(ext[HEAD : HEAD + SEG, :CHUNK].astype(jnp.float32))[:RESP]
    arrived(final.at[pl.ds(0, tm - 1)], FINAL)
    for c in range(4):
        avg_ref[:, c * CHUNK : (c + 1) * CHUNK] = final[4 * b + c].astype(jnp.float32)
    stacked = jnp.concatenate(
        [
            jnp.concatenate([final[lag * 8 + c] for c in range(8)], axis=1)
            for lag in range(LAGS)
        ],
        axis=0,
    )
    forecast = lax.dot_general(stacked, ext[...], NT, preferred_element_type=jnp.float32)
    residual = normed
    for lag in range(LAGS):
        begin = HEAD - 1 - lag
        turned = pltpu.roll(forecast[lag * RESP : (lag + 1) * RESP], WINDOW - begin, 1)
        residual = residual - turned[:, :SEG]
    res_ref[...] = residual

    left(power.at[pl.ds(0, tm - 1)], POWER)
    left(halo, HALO)
    left(sup.at[pl.ds(0, boots - 1)], SUPPORT)
    left(outgoing.at[pl.ds(0, tm - 1)], SCATTER + ITERS - 1)
    left(gathered.at[pl.ds(0, tm - 1)], GATHER + ITERS - 2)
    left(norms.at[pl.ds(0, tm - 1)], NORMS)
    left(zx.at[pl.ds(0, boots - 1)], BOOTS)
    left(final.at[pl.ds(0, tm - 1)], FINAL)


def per_device(recording, starts, lengths, support):
    tm = lax.axis_size("tm")
    boots = lax.axis_size("boot")
    vmem = pl.BlockSpec(memory_space=pltpu.VMEM)
    smem = pl.BlockSpec(memory_space=pltpu.SMEM)
    return pl.pallas_call(
        functools.partial(kernel, tm, boots),
        out_shape=(
            jax.ShapeDtypeStruct((RESP, FEAT // boots), jnp.float32),
            jax.ShapeDtypeStruct((RESP, SEG), jnp.float32),
        ),
        in_specs=[vmem, smem, smem, vmem],
        out_specs=(vmem, vmem),
        scratch_shapes=[
            pltpu.VMEM((HEAD, CHANNELS), jnp.bfloat16),
            pltpu.VMEM((tm, 1, CHANNELS), jnp.float32),
            pltpu.VMEM((boots, boots, FEAT // boots), jnp.int32),
            pltpu.VMEM((WINDOW, CHANNELS), jnp.bfloat16),
            pltpu.VMEM((CAP, FEAT), jnp.bfloat16),
            pltpu.VMEM((RESP, FEAT), jnp.float32),
            pltpu.VMEM((RESP, FEAT), jnp.float32),
            pltpu.VMEM((RESP, FEAT), jnp.float32),
            pltpu.VMEM((RESP, FEAT), jnp.bfloat16),
            pltpu.VMEM((tm, RESP, CHUNK), jnp.bfloat16),
            pltpu.VMEM((tm - 1, RESP, CHUNK), jnp.bfloat16),
            pltpu.VMEM((tm, RESP, CHUNK), jnp.bfloat16),
            pltpu.VMEM((tm, 1, CHUNK), jnp.float32),
            pltpu.VMEM((boots, RESP, CHUNK), jnp.bfloat16),
            pltpu.VMEM((tm, RESP, CHUNK), jnp.bfloat16),
            pltpu.SemaphoreType.DMA((PHASES,)),
            pltpu.SemaphoreType.DMA((PHASES,)),
        ],
        compiler_params=pltpu.CompilerParams(
            collective_id=0, has_side_effects=True, vmem_limit_bytes=48 * 1024 * 1024
        ),
    )(recording, starts, lengths, support)


def solution(mesh):
    in_specs = (P("tm", None), P("boot", "tm"), P("boot", "tm"), P(None, "boot"))
    out_specs = (P(None, "boot"), P(None, "tm"))
    return jax.shard_map(
        per_device, mesh=mesh, in_specs=in_specs, out_specs=out_specs, check_vma=False
    )
```

```python
import functools

import jax
import jax.numpy as jnp
from jax import lax
from jax.experimental import pallas as pl
from jax.experimental.pallas import tpu as pltpu
from jax.sharding import PartitionSpec as P

CHANNELS = 1024
LAGS = 4
FEAT = LAGS * CHANNELS
RESP = 32
NBLK = 6
CAP = 384
SEG = 512
ITERS = 3
CHEB = 5
HEAD = 16
WINDOW = 640
CHUNK = 128

RHO = 4.0
SHRINK = 0.75
EPSILON = 1e-05

HIGHEST = lax.Precision.HIGHEST
NT = (((1,), (1,)), ((), ()))
HALO, POWER, SUPPORT, SCATTER, GATHER, NORMS, BOOTS, FINAL = 0, 1, 2, 3, 6, 8, 9, 10
PHASES = 11


def chebyshev(gram, rhs, bound):
    theta = RHO + 0.5 * bound
    delta = 0.5 * bound
    sigma = theta / delta
    total = jnp.zeros_like(rhs)
    remain = rhs
    factor = 1.0 / sigma
    update = rhs / theta
    for count in range(CHEB):
        total = total + update
        if count + 1 < CHEB:
            applied = RHO * update + jnp.dot(
                update, gram, precision=HIGHEST, preferred_element_type=jnp.float32
            )
            remain = remain - applied
            after = 1.0 / (2.0 * sigma - factor)
            update = after * factor * update + 2.0 * after / delta * remain
            factor = after
    return total


def chebyshev_terms(bound):
    theta = RHO + 0.5 * bound
    delta = 0.5 * bound
    sigma = theta / delta
    nought = jnp.zeros_like(bound)
    total = [nought] * CHEB
    remain = [jnp.ones_like(bound)] + [nought] * (CHEB - 1)
    factor = 1.0 / sigma
    update = [term / theta for term in remain]
    for count in range(CHEB):
        total = [a + b for a, b in zip(total, update)]
        if count + 1 < CHEB:
            applied = [
                theta * update[k] + (delta * update[k - 1] if k else 0.0)
                for k in range(CHEB)
            ]
            remain = [a - b for a, b in zip(remain, applied)]
            after = 1.0 / (2.0 * sigma - factor)
            update = [
                after * factor * d + 2.0 * after / delta * r
                for d, r in zip(update, remain)
            ]
            factor = after
    return total, delta


def far_first():
    offsets = [(d, p, a, c) for d in range(4) for p in range(2) for a in range(2) for c in range(2)]
    hops = {o: min(o[0], 4 - o[0]) + (2 if o[1] > o[2] else o[1] | o[2]) for o in offsets}
    return sorted(offsets[1:], key=lambda o: -hops[o])


def kernel(
    tm,
    boots,
    rec_hbm,
    starts_hbm,
    lengths_hbm,
    support_hbm,
    avg_ref,
    res_ref,
    rec,
    starts_ref,
    lengths_ref,
    halo,
    power,
    sup,
    ext,
    design,
    cross,
    v,
    z,
    tb,
    solver,
    flat,
    outgoing,
    incoming,
    gathered,
    norms,
    zx,
    final,
    send_sem,
    recv_sem,
    local_sem,
):
    b = lax.axis_index("boot")
    me = lax.axis_index("tm")
    x, y, core = me // 8, lax.rem(me // 2, 4), lax.rem(me, 2)
    offsets = far_first()

    def tm_at(o):
        pair, place = lax.rem(y // 2 + o[1], 2), lax.rem(lax.rem(y, 2) + o[2], 2)
        return lax.rem(x + o[0], 4) * 8 + pair * 4 + place * 2 + lax.rem(core + o[3], 2)

    def tm_peer(i):
        return lax.rem(me + i, tm)

    def boot_peer(i):
        return lax.rem(b + i, boots)

    barrier = pltpu.get_barrier_semaphore()

    @pl.loop(1, tm)
    def _(i):
        pl.semaphore_signal(
            barrier, inc=1, device_id={"tm": tm_peer(i)}, device_id_type=pl.DeviceIdType.MESH
        )

    @pl.loop(1, boots)
    def _(i):
        pl.semaphore_signal(
            barrier, inc=1, device_id={"boot": boot_peer(i)}, device_id_type=pl.DeviceIdType.MESH
        )

    def fetch(src, dst, k):
        copy = pltpu.make_async_copy(src, dst, local_sem.at[k])
        copy.start()
        return copy

    rec_copy = fetch(rec_hbm, rec, 0)
    starts_copy = fetch(starts_hbm, starts_ref, 1)
    lengths_copy = fetch(lengths_hbm, lengths_ref, 2)
    support_copy = fetch(support_hbm, sup.at[b], 3)

    def send(src, dst, phase, target):
        pltpu.make_async_remote_copy(
            src_ref=src,
            dst_ref=dst,
            send_sem=send_sem.at[phase],
            recv_sem=recv_sem.at[phase],
            device_id=target,
            device_id_type=pl.DeviceIdType.MESH,
        ).start()

    def to_tm(src, dst, phase):
        for o in offsets:
            send(src, dst, phase, {"tm": tm_at(o)})

    def to_boots(src, dst, phase):
        for i in (4, 3, 5, 2, 6, 1, 7):
            send(src, dst, phase, {"boot": boot_peer(i)})

    def arrived(ref, phase):
        pltpu.make_async_copy(ref, ref, recv_sem.at[phase]).wait()

    def left(ref, phase):
        pltpu.make_async_copy(ref, ref, send_sem.at[phase]).wait()

    rec_copy.wait()
    acc = jnp.zeros((8, CHANNELS), jnp.float32)

    def add_rows(k, acc):
        block = rec[pl.ds(pl.multiple_of(k * 16, 16), 16), :].astype(jnp.float32)
        block = block * block
        return acc + block[:8] + block[8:]

    acc = lax.fori_loop(0, SEG // 16, add_rows, acc)
    power[me] = jnp.sum(acc, axis=0, keepdims=True)

    starts_copy.wait()
    lengths_copy.wait()
    row = lax.broadcasted_iota(jnp.int32, (CAP, CHUNK), 0)
    place = jnp.full((CAP, CHUNK), -4 * SEG, jnp.int32)
    offset = jnp.int32(0)
    for k in range(NBLK):
        length = lengths_ref[0, k]
        inside = (row >= offset) & (row < offset + length)
        place = jnp.where(inside, row + (starts_ref[0, k] - offset), place)
        offset = offset + length
    lane = lax.broadcasted_iota(jnp.int32, (CAP, CHUNK), 1)

    def picks(back, width):
        return jnp.concatenate(
            [
                jnp.where(place - back == lane + c * CHUNK, 1.0, 0.0).astype(jnp.bfloat16)
                for c in range(width // CHUNK)
            ],
            axis=1,
        )

    def raw_rows(lag):
        pick = picks(1 + lag, SEG)
        for part in range(4):
            at = lag * CHANNELS + part * 256
            design[:, at : at + 256] = jnp.dot(
                pick, rec[:, part * 256 : (part + 1) * 256], preferred_element_type=jnp.float32
            ).astype(jnp.bfloat16)

    support_copy.wait()
    raw_rows(0)
    pl.semaphore_wait(barrier, tm + boots - 2)
    send(rec_hbm.at[pl.ds(SEG - HEAD, HEAD)], halo, HALO, {"tm": tm_peer(1)})
    to_tm(power.at[me], power.at[me], POWER)
    to_boots(support_hbm, sup.at[b], SUPPORT)
    raw_rows(1)
    raw_rows(2)
    raw_rows(3)
    answer = jnp.dot(picks(0, SEG), rec[:, :CHUNK], preferred_element_type=jnp.float32)
    arrived(halo, HALO)
    before = halo[...]
    before = jnp.where(me == 0, jnp.zeros_like(before), before)
    behind = lane - HEAD
    for lag in range(LAGS):
        cols = slice(lag * CHANNELS, (lag + 1) * CHANNELS)
        reach = jnp.where(place - 1 - lag == behind, 1.0, 0.0).astype(jnp.bfloat16)[:, :HEAD]
        extra = jnp.dot(reach, before, preferred_element_type=jnp.float32)
        design[:, cols] = (design[:, cols].astype(jnp.float32) + extra).astype(jnp.bfloat16)
    arrived(power.at[pl.ds(0, tm - 1)], POWER)
    total = jnp.sum(power[...], axis=0)
    scale = 1.0 / jnp.sqrt(total / (SEG * tm) + EPSILON)

    answer = (answer * scale[:, :CHUNK]).astype(jnp.bfloat16).astype(jnp.float32)
    answer = jnp.transpose(answer)[:RESP].astype(jnp.bfloat16)
    gram = jnp.zeros((CAP, CAP), jnp.float32)
    for lag in range(LAGS):
        cols = slice(lag * CHANNELS, (lag + 1) * CHANNELS)
        piece = (design[:, cols].astype(jnp.float32) * scale).astype(jnp.bfloat16)
        design[:, cols] = piece
        gram = gram + lax.dot_general(piece, piece, NT, preferred_element_type=jnp.float32)
        fit = jnp.dot(answer, piece, preferred_element_type=jnp.float32) * (1.0 / CAP)
        cross[:, cols] = fit
        tb[:, cols] = fit.astype(jnp.bfloat16)
    gram = gram * (1.0 / CAP)
    solver[...] = gram
    bound = jnp.sqrt(jnp.sum(jnp.sum(gram * gram, axis=1, keepdims=True), axis=0, keepdims=True))

    mine = pl.ds(pl.multiple_of(me * CHUNK, CHUNK), CHUNK)
    for it in range(ITERS):
        projected = jnp.zeros((RESP, CAP), jnp.float32)
        for part in range(8):
            cols = slice(part * 512, (part + 1) * 512)
            projected = projected + lax.dot_general(
                tb[:, cols], design[:, cols], NT, preferred_element_type=jnp.float32
            )
        projected = projected * (1.0 / CAP)
        if it == 0:
            flat[...] = projected
            weights = chebyshev(solver[...], projected, bound)
            flat[...] = weights
        else:
            weights = jnp.dot(
                projected, solver[...], precision=HIGHEST, preferred_element_type=jnp.float32
            )
        weights = weights.astype(jnp.bfloat16)
        if it:
            left(outgoing.at[pl.ds(0, tm - 1)], SCATTER + it - 1)
        for dx, dp in ((2, 1), (2, 0), (1, 1), (3, 1), (1, 0), (3, 0), (0, 1), (0, 0)):
            group = lax.rem(x + dx, 4) * 2 + lax.rem(y // 2 + dp, 2)
            cols = pl.ds(pl.multiple_of(group * 512, 512), 512)
            back = jnp.dot(weights, design[:, cols], preferred_element_type=jnp.float32)
            value = (cross[:, cols] - back) * (1.0 / RHO)
            v[:, cols] = value
            for c in range(4):
                outgoing[group * 4 + c] = value[:, c * CHUNK : (c + 1) * CHUNK].astype(jnp.bfloat16)
            for slot, o in enumerate(offsets):
                if o[:2] == (dx, dp):
                    peer = tm_at(o)
                    send(outgoing.at[peer], incoming.at[slot], SCATTER + it, {"tm": peer})

        if it == 0:
            terms, delta = chebyshev_terms(bound)
            ri = lax.broadcasted_iota(jnp.int32, (CAP, CAP), 0)
            ci = lax.broadcasted_iota(jnp.int32, (CAP, CAP), 1)
            eye = jnp.where(ri == ci, 1.0, 0.0)
            x1 = solver[...] * (1.0 / delta) - eye
            x2 = jnp.dot(x1, x1, precision=HIGHEST, preferred_element_type=jnp.float32)
            solver[...] = (
                terms[0] * eye
                + terms[1] * x1
                + terms[2] * x2
                + jnp.dot(
                    x2,
                    terms[3] * x1 + terms[4] * x2,
                    precision=HIGHEST,
                    preferred_element_type=jnp.float32,
                )
            )

            def scale_rows(k, carry):
                at = pl.multiple_of(k * 16, 16)
                block = rec[pl.ds(at, 16), :].astype(jnp.float32) * scale
                ext[pl.ds(pl.multiple_of(at + HEAD, 16), 16), :] = block.astype(jnp.bfloat16)
                return carry

            lax.fori_loop(0, SEG // 16, scale_rows, 0)
            ext[0:HEAD, :] = (before.astype(jnp.float32) * scale).astype(jnp.bfloat16)
            ext[HEAD + SEG :, :] = jnp.zeros((WINDOW - HEAD - SEG, CHANNELS), jnp.bfloat16)
            normed = ext[HEAD : HEAD + SEG, :CHUNK].astype(jnp.float32)
            res_ref[...] = jnp.transpose(normed)[:RESP]

        arrived(incoming, SCATTER + it)
        mean = v[:, mine]
        for i in range(tm - 1):
            mean = mean + incoming[i].astype(jnp.float32)
        mean = mean * (1.0 / tm)
        if it:
            mean = mean + z[:, mine]
        if it + 1 < ITERS:
            if it:
                left(gathered.at[pl.ds(0, tm - 1)], GATHER + it - 1)
            gathered[me] = mean.astype(jnp.bfloat16)
            to_tm(gathered.at[me], gathered.at[me], GATHER + it)
            arrived(gathered.at[pl.ds(0, tm - 1)], GATHER + it)
            lengths = []
            for c in range(tm):
                block = gathered[c].astype(jnp.float32)
                lengths.append(jnp.sqrt(jnp.sum(block * block, axis=0, keepdims=True)))
            level = (
                jnp.sum(functools.reduce(jnp.add, lengths), axis=1, keepdims=True)
                * (SHRINK / FEAT)
            )
            for c in range(tm):
                cols = slice(c * CHUNK, (c + 1) * CHUNK)
                factor = jnp.maximum(lengths[c] - level, 0.0) / jnp.maximum(lengths[c], level)
                fresh = gathered[c].astype(jnp.float32) * factor
                dual = v[:, cols] - fresh
                if it:
                    dual = dual + z[:, cols]
                z[:, cols] = fresh
                tb[:, cols] = (cross[:, cols] + RHO * (fresh - dual)).astype(jnp.bfloat16)

    length = jnp.sqrt(jnp.sum(mean * mean, axis=0, keepdims=True))
    norms[me] = length
    to_tm(norms.at[me], norms.at[me], NORMS)
    arrived(norms.at[pl.ds(0, tm - 1)], NORMS)
    level = jnp.sum(jnp.sum(norms[...], axis=0), axis=1, keepdims=True) * (SHRINK / FEAT)
    factor = jnp.maximum(length - level, 0.0) / jnp.maximum(length, level)
    zx[b] = (mean * factor).astype(jnp.bfloat16)
    to_boots(zx.at[b], zx.at[b], BOOTS)
    arrived(sup.at[pl.ds(0, boots - 1)], SUPPORT)
    quarter = pl.ds(pl.multiple_of(lax.rem(me, 4) * CHUNK, CHUNK), CHUNK)
    chosen = sup[me // 4, :, quarter].astype(jnp.float32)
    tally = jnp.maximum(jnp.sum(chosen, axis=0, keepdims=True), 1.0)
    arrived(zx.at[pl.ds(0, boots - 1)], BOOTS)
    average = jnp.zeros((RESP, CHUNK), jnp.float32)
    for k in range(boots):
        average = average + chosen[k : k + 1] * zx[k].astype(jnp.float32)
    average = average / tally
    final[me] = average.astype(jnp.bfloat16)
    to_tm(final.at[me], final.at[me], FINAL)
    arrived(final.at[pl.ds(0, tm - 1)], FINAL)
    for c in range(4):
        avg_ref[:, c * CHUNK : (c + 1) * CHUNK] = final[4 * b + c].astype(jnp.float32)
    stacked = jnp.concatenate(
        [
            jnp.concatenate([final[lag * 8 + c] for c in range(8)], axis=1)
            for lag in range(LAGS)
        ],
        axis=0,
    )
    forecast = lax.dot_general(stacked, ext[...], NT, preferred_element_type=jnp.float32)
    residual = res_ref[...]
    for lag in range(LAGS):
        begin = HEAD - 1 - lag
        turned = pltpu.roll(forecast[lag * RESP : (lag + 1) * RESP], WINDOW - begin, 1)
        residual = residual - turned[:, :SEG]
    res_ref[...] = residual

    left(power.at[pl.ds(0, tm - 1)], POWER)
    left(halo, HALO)
    left(sup.at[pl.ds(0, boots - 1)], SUPPORT)
    left(outgoing.at[pl.ds(0, tm - 1)], SCATTER + ITERS - 1)
    left(gathered.at[pl.ds(0, tm - 1)], GATHER + ITERS - 2)
    left(norms.at[pl.ds(0, tm - 1)], NORMS)
    left(zx.at[pl.ds(0, boots - 1)], BOOTS)
    left(final.at[pl.ds(0, tm - 1)], FINAL)


def per_device(recording, starts, lengths, support):
    tm = lax.axis_size("tm")
    boots = lax.axis_size("boot")
    vmem = pl.BlockSpec(memory_space=pltpu.VMEM)
    anywhere = pl.BlockSpec(memory_space=pl.ANY)
    return pl.pallas_call(
        functools.partial(kernel, tm, boots),
        out_shape=(
            jax.ShapeDtypeStruct((RESP, FEAT // boots), jnp.float32),
            jax.ShapeDtypeStruct((RESP, SEG), jnp.float32),
        ),
        in_specs=[anywhere] * 4,
        out_specs=(vmem, vmem),
        scratch_shapes=[
            pltpu.VMEM((SEG, CHANNELS), jnp.bfloat16),
            pltpu.SMEM((1, NBLK), jnp.int32),
            pltpu.SMEM((1, NBLK), jnp.int32),
            pltpu.VMEM((HEAD, CHANNELS), jnp.bfloat16),
            pltpu.VMEM((tm, 1, CHANNELS), jnp.float32),
            pltpu.VMEM((boots, boots, FEAT // boots), jnp.int32),
            pltpu.VMEM((WINDOW, CHANNELS), jnp.bfloat16),
            pltpu.VMEM((CAP, FEAT), jnp.bfloat16),
            pltpu.VMEM((RESP, FEAT), jnp.float32),
            pltpu.VMEM((RESP, FEAT), jnp.float32),
            pltpu.VMEM((RESP, FEAT), jnp.float32),
            pltpu.VMEM((RESP, FEAT), jnp.bfloat16),
            pltpu.VMEM((CAP, CAP), jnp.float32),
            pltpu.VMEM((RESP, CAP), jnp.float32),
            pltpu.VMEM((tm, RESP, CHUNK), jnp.bfloat16),
            pltpu.VMEM((tm - 1, RESP, CHUNK), jnp.bfloat16),
            pltpu.VMEM((tm, RESP, CHUNK), jnp.bfloat16),
            pltpu.VMEM((tm, 1, CHUNK), jnp.float32),
            pltpu.VMEM((boots, RESP, CHUNK), jnp.bfloat16),
            pltpu.VMEM((tm, RESP, CHUNK), jnp.bfloat16),
            pltpu.SemaphoreType.DMA((PHASES,)),
            pltpu.SemaphoreType.DMA((PHASES,)),
            pltpu.SemaphoreType.DMA((4,)),
        ],
        compiler_params=pltpu.CompilerParams(
            collective_id=0, has_side_effects=True, vmem_limit_bytes=48 * 1024 * 1024
        ),
    )(recording, starts, lengths, support)


def solution(mesh):
    in_specs = (P("tm", None), P("boot", "tm"), P("boot", "tm"), P(None, "boot"))
    out_specs = (P(None, "boot"), P(None, "tm"))
    return jax.shard_map(
        per_device, mesh=mesh, in_specs=in_specs, out_specs=out_specs, check_vma=False
    )
```

```python
import functools

import jax
import jax.numpy as jnp
from jax import lax
from jax.experimental import pallas as pl
from jax.experimental.pallas import tpu as pltpu
from jax.sharding import PartitionSpec as P

CHANNELS = 1024
LAGS = 4
FEAT = LAGS * CHANNELS
RESP = 32
NBLK = 6
CAP = 384
SEG = 512
ITERS = 3
CHEB = 5
HEAD = 16
WINDOW = 640
CHUNK = 128

RHO = 4.0
SHRINK = 0.75
EPSILON = 1e-05

HIGHEST = lax.Precision.HIGHEST
NT = (((1,), (1,)), ((), ()))
HALO, POWER, SUPPORT, SCATTER, GATHER, NORMS, BOOTS, FINAL = 0, 1, 2, 3, 6, 8, 9, 10
PHASES = 11


def chebyshev(gram, rhs, bound):
    theta = RHO + 0.5 * bound
    delta = 0.5 * bound
    sigma = theta / delta
    total = jnp.zeros_like(rhs)
    remain = rhs
    factor = 1.0 / sigma
    update = rhs / theta
    for count in range(CHEB):
        total = total + update
        if count + 1 < CHEB:
            applied = RHO * update + jnp.dot(
                update, gram, precision=HIGHEST, preferred_element_type=jnp.float32
            )
            remain = remain - applied
            after = 1.0 / (2.0 * sigma - factor)
            update = after * factor * update + 2.0 * after / delta * remain
            factor = after
    return total


def chebyshev_terms(bound):
    theta = RHO + 0.5 * bound
    delta = 0.5 * bound
    sigma = theta / delta
    nought = jnp.zeros_like(bound)
    total = [nought] * CHEB
    remain = [jnp.ones_like(bound)] + [nought] * (CHEB - 1)
    factor = 1.0 / sigma
    update = [term / theta for term in remain]
    for count in range(CHEB):
        total = [a + b for a, b in zip(total, update)]
        if count + 1 < CHEB:
            applied = [
                theta * update[k] + (delta * update[k - 1] if k else 0.0)
                for k in range(CHEB)
            ]
            remain = [a - b for a, b in zip(remain, applied)]
            after = 1.0 / (2.0 * sigma - factor)
            update = [
                after * factor * d + 2.0 * after / delta * r
                for d, r in zip(update, remain)
            ]
            factor = after
    return total, delta


def far_first():
    offsets = [(d, p, a, c) for d in range(4) for p in range(2) for a in range(2) for c in range(2)]
    hops = {o: min(o[0], 4 - o[0]) + (2 if o[1] > o[2] else o[1] | o[2]) for o in offsets}
    return sorted(offsets[1:], key=lambda o: -hops[o])


def kernel(
    tm,
    boots,
    rec_hbm,
    starts_hbm,
    lengths_hbm,
    support_hbm,
    packed,
    rec,
    starts_ref,
    lengths_ref,
    halo,
    power,
    sup,
    ext,
    design,
    cross,
    v,
    z,
    tb,
    solver,
    outgoing,
    incoming,
    gathered,
    norms,
    zx,
    final,
    send_sem,
    recv_sem,
    local_sem,
):
    b = lax.axis_index("boot")
    me = lax.axis_index("tm")
    x, y, core = me // 8, lax.rem(me // 2, 4), lax.rem(me, 2)
    offsets = far_first()

    def tm_at(o):
        pair, place = lax.rem(y // 2 + o[1], 2), lax.rem(lax.rem(y, 2) + o[2], 2)
        return lax.rem(x + o[0], 4) * 8 + pair * 4 + place * 2 + lax.rem(core + o[3], 2)

    def tm_peer(i):
        return lax.rem(me + i, tm)

    def boot_peer(i):
        return lax.rem(b + i, boots)

    barrier = pltpu.get_barrier_semaphore()

    @pl.loop(1, tm)
    def _(i):
        pl.semaphore_signal(
            barrier, inc=1, device_id={"tm": tm_peer(i)}, device_id_type=pl.DeviceIdType.MESH
        )

    @pl.loop(1, boots)
    def _(i):
        pl.semaphore_signal(
            barrier, inc=1, device_id={"boot": boot_peer(i)}, device_id_type=pl.DeviceIdType.MESH
        )

    def fetch(src, dst, k):
        copy = pltpu.make_async_copy(src, dst, local_sem.at[k])
        copy.start()
        return copy

    rec_copy = fetch(rec_hbm, rec, 0)
    starts_copy = fetch(starts_hbm, starts_ref, 1)
    lengths_copy = fetch(lengths_hbm, lengths_ref, 2)
    support_copy = fetch(support_hbm, sup.at[b], 3)

    def send(src, dst, phase, target):
        pltpu.make_async_remote_copy(
            src_ref=src,
            dst_ref=dst,
            send_sem=send_sem.at[phase],
            recv_sem=recv_sem.at[phase],
            device_id=target,
            device_id_type=pl.DeviceIdType.MESH,
        ).start()

    def to_tm(src, dst, phase):
        for o in offsets:
            send(src, dst, phase, {"tm": tm_at(o)})

    def to_boots(src, dst, phase):
        for i in (4, 3, 5, 2, 6, 1, 7):
            send(src, dst, phase, {"boot": boot_peer(i)})

    def arrived(ref, phase):
        pltpu.make_async_copy(ref, ref, recv_sem.at[phase]).wait()

    def left(ref, phase):
        pltpu.make_async_copy(ref, ref, send_sem.at[phase]).wait()

    rec_copy.wait()
    acc = jnp.zeros((8, CHANNELS), jnp.float32)

    def add_rows(k, acc):
        block = rec[pl.ds(pl.multiple_of(k * 16, 16), 16), :].astype(jnp.float32)
        block = block * block
        return acc + block[:8] + block[8:]

    acc = lax.fori_loop(0, SEG // 16, add_rows, acc)
    power[me] = jnp.sum(acc, axis=0, keepdims=True)

    starts_copy.wait()
    lengths_copy.wait()
    row = lax.broadcasted_iota(jnp.int32, (CAP, CHUNK), 0)
    place = jnp.full((CAP, CHUNK), -4 * SEG, jnp.int32)
    offset = jnp.int32(0)
    for k in range(NBLK):
        length = lengths_ref[0, k]
        inside = (row >= offset) & (row < offset + length)
        place = jnp.where(inside, row + (starts_ref[0, k] - offset), place)
        offset = offset + length
    lane = lax.broadcasted_iota(jnp.int32, (CAP, CHUNK), 1)

    def picks(back, width):
        return jnp.concatenate(
            [
                jnp.where(place - back == lane + c * CHUNK, 1.0, 0.0).astype(jnp.bfloat16)
                for c in range(width // CHUNK)
            ],
            axis=1,
        )

    def raw_rows(lag):
        pick = picks(1 + lag, SEG)
        for part in range(4):
            at = lag * CHANNELS + part * 256
            design[:, at : at + 256] = jnp.dot(
                pick, rec[:, part * 256 : (part + 1) * 256], preferred_element_type=jnp.float32
            ).astype(jnp.bfloat16)

    support_copy.wait()
    raw_rows(0)
    pl.semaphore_wait(barrier, tm + boots - 2)
    send(rec_hbm.at[pl.ds(SEG - HEAD, HEAD)], halo, HALO, {"tm": tm_peer(1)})
    to_tm(power.at[me], power.at[me], POWER)
    to_boots(support_hbm, sup.at[b], SUPPORT)
    raw_rows(1)
    raw_rows(2)
    raw_rows(3)
    answer = jnp.dot(picks(0, SEG), rec[:, :CHUNK], preferred_element_type=jnp.float32)
    arrived(halo, HALO)
    before = halo[...]
    before = jnp.where(me == 0, jnp.zeros_like(before), before)
    behind = lane - HEAD
    for lag in range(LAGS):
        cols = slice(lag * CHANNELS, (lag + 1) * CHANNELS)
        reach = jnp.where(place - 1 - lag == behind, 1.0, 0.0).astype(jnp.bfloat16)[:, :HEAD]
        extra = jnp.dot(reach, before, preferred_element_type=jnp.float32)
        design[:, cols] = (design[:, cols].astype(jnp.float32) + extra).astype(jnp.bfloat16)
    arrived(power.at[pl.ds(0, tm - 1)], POWER)
    total = jnp.sum(power[...], axis=0)
    scale = 1.0 / jnp.sqrt(total / (SEG * tm) + EPSILON)

    answer = (answer * scale[:, :CHUNK]).astype(jnp.bfloat16).astype(jnp.float32)
    answer = jnp.transpose(answer)[:RESP].astype(jnp.bfloat16)
    gram = jnp.zeros((CAP, CAP), jnp.float32)
    for lag in range(LAGS):
        cols = slice(lag * CHANNELS, (lag + 1) * CHANNELS)
        piece = (design[:, cols].astype(jnp.float32) * scale).astype(jnp.bfloat16)
        design[:, cols] = piece
        gram = gram + lax.dot_general(piece, piece, NT, preferred_element_type=jnp.float32)
        fit = jnp.dot(answer, piece, preferred_element_type=jnp.float32) * (1.0 / CAP)
        cross[:, cols] = fit
        tb[:, cols] = fit.astype(jnp.bfloat16)
    gram = gram * (1.0 / CAP)
    solver[...] = gram
    bound = jnp.sqrt(jnp.sum(jnp.sum(gram * gram, axis=1, keepdims=True), axis=0, keepdims=True))

    mine = pl.ds(pl.multiple_of(me * CHUNK, CHUNK), CHUNK)
    for it in range(ITERS):
        projected = jnp.zeros((RESP, CAP), jnp.float32)
        for part in range(8):
            cols = slice(part * 512, (part + 1) * 512)
            projected = projected + lax.dot_general(
                tb[:, cols], design[:, cols], NT, preferred_element_type=jnp.float32
            )
        projected = projected * (1.0 / CAP)
        if it == 0:
            weights = chebyshev(solver[...], projected, bound)
        else:
            weights = jnp.dot(
                projected, solver[...], precision=HIGHEST, preferred_element_type=jnp.float32
            )
        weights = weights.astype(jnp.bfloat16)
        if it:
            left(outgoing.at[pl.ds(0, tm - 1)], SCATTER + it - 1)
        for dx, dp in ((2, 1), (2, 0), (1, 1), (3, 1), (1, 0), (3, 0), (0, 1), (0, 0)):
            group = lax.rem(x + dx, 4) * 2 + lax.rem(y // 2 + dp, 2)
            cols = pl.ds(pl.multiple_of(group * 512, 512), 512)
            back = jnp.dot(weights, design[:, cols], preferred_element_type=jnp.float32)
            value = (cross[:, cols] - back) * (1.0 / RHO)
            v[:, cols] = value
            for c in range(4):
                outgoing[group * 4 + c] = value[:, c * CHUNK : (c + 1) * CHUNK].astype(jnp.bfloat16)
            for slot, o in enumerate(offsets):
                if o[:2] == (dx, dp):
                    peer = tm_at(o)
                    send(outgoing.at[peer], incoming.at[slot], SCATTER + it, {"tm": peer})

        if it == 0:
            terms, delta = chebyshev_terms(bound)
            ri = lax.broadcasted_iota(jnp.int32, (CAP, CAP), 0)
            ci = lax.broadcasted_iota(jnp.int32, (CAP, CAP), 1)
            eye = jnp.where(ri == ci, 1.0, 0.0)
            x1 = solver[...] * (1.0 / delta) - eye
            x2 = jnp.dot(x1, x1, precision=HIGHEST, preferred_element_type=jnp.float32)
            solver[...] = (
                terms[0] * eye
                + terms[1] * x1
                + terms[2] * x2
                + jnp.dot(
                    x2,
                    terms[3] * x1 + terms[4] * x2,
                    precision=HIGHEST,
                    preferred_element_type=jnp.float32,
                )
            )

            def scale_rows(k, carry):
                at = pl.multiple_of(k * 16, 16)
                block = rec[pl.ds(at, 16), :].astype(jnp.float32) * scale
                ext[pl.ds(pl.multiple_of(at + HEAD, 16), 16), :] = block.astype(jnp.bfloat16)
                return carry

            lax.fori_loop(0, SEG // 16, scale_rows, 0)
            ext[0:HEAD, :] = (before.astype(jnp.float32) * scale).astype(jnp.bfloat16)
            ext[HEAD + SEG :, :] = jnp.zeros((WINDOW - HEAD - SEG, CHANNELS), jnp.bfloat16)
            normed = ext[HEAD : HEAD + SEG, :CHUNK].astype(jnp.float32)
            packed[:RESP] = jnp.transpose(normed)[:RESP]

        arrived(incoming, SCATTER + it)
        mean = v[:, mine]
        for i in range(tm - 1):
            mean = mean + incoming[i].astype(jnp.float32)
        mean = mean * (1.0 / tm)
        if it:
            mean = mean + z[:, mine]
        if it + 1 < ITERS:
            if it:
                left(gathered.at[pl.ds(0, tm - 1)], GATHER + it - 1)
            gathered[me] = mean.astype(jnp.bfloat16)
            to_tm(gathered.at[me], gathered.at[me], GATHER + it)
            arrived(gathered.at[pl.ds(0, tm - 1)], GATHER + it)
            lengths = []
            for c in range(tm):
                block = gathered[c].astype(jnp.float32)
                lengths.append(jnp.sqrt(jnp.sum(block * block, axis=0, keepdims=True)))
            level = (
                jnp.sum(functools.reduce(jnp.add, lengths), axis=1, keepdims=True)
                * (SHRINK / FEAT)
            )
            for c in range(tm):
                cols = slice(c * CHUNK, (c + 1) * CHUNK)
                factor = jnp.maximum(lengths[c] - level, 0.0) / jnp.maximum(lengths[c], level)
                fresh = gathered[c].astype(jnp.float32) * factor
                dual = v[:, cols] - fresh
                if it:
                    dual = dual + z[:, cols]
                z[:, cols] = fresh
                tb[:, cols] = (cross[:, cols] + RHO * (fresh - dual)).astype(jnp.bfloat16)

    length = jnp.sqrt(jnp.sum(mean * mean, axis=0, keepdims=True))
    norms[me] = length
    to_tm(norms.at[me], norms.at[me], NORMS)
    arrived(norms.at[pl.ds(0, tm - 1)], NORMS)
    level = jnp.sum(jnp.sum(norms[...], axis=0), axis=1, keepdims=True) * (SHRINK / FEAT)
    factor = jnp.maximum(length - level, 0.0) / jnp.maximum(length, level)
    zx[b] = (mean * factor).astype(jnp.bfloat16)
    to_boots(zx.at[b], zx.at[b], BOOTS)
    arrived(sup.at[pl.ds(0, boots - 1)], SUPPORT)
    quarter = pl.ds(pl.multiple_of(lax.rem(me, 4) * CHUNK, CHUNK), CHUNK)
    chosen = sup[me // 4, :, quarter].astype(jnp.float32)
    tally = jnp.maximum(jnp.sum(chosen, axis=0, keepdims=True), 1.0)
    arrived(zx.at[pl.ds(0, boots - 1)], BOOTS)
    average = jnp.zeros((RESP, CHUNK), jnp.float32)
    for k in range(boots):
        average = average + chosen[k : k + 1] * zx[k].astype(jnp.float32)
    average = average / tally
    final[me] = average.astype(jnp.bfloat16)
    to_tm(final.at[me], final.at[me], FINAL)
    arrived(final.at[pl.ds(0, tm - 1)], FINAL)
    for c in range(4):
        packed[2 * RESP :, c * CHUNK : (c + 1) * CHUNK] = final[4 * b + c].astype(jnp.float32)
    stacked = jnp.concatenate(
        [
            jnp.concatenate([final[lag * 8 + c] for c in range(8)], axis=1)
            for lag in range(LAGS)
        ],
        axis=0,
    )
    forecast = lax.dot_general(stacked, ext[...], NT, preferred_element_type=jnp.float32)
    told = jnp.zeros((RESP, SEG), jnp.float32)
    for lag in range(LAGS):
        begin = HEAD - 1 - lag
        turned = pltpu.roll(forecast[lag * RESP : (lag + 1) * RESP], WINDOW - begin, 1)
        told = told + turned[:, :SEG]
    packed[RESP : 2 * RESP] = told

    left(power.at[pl.ds(0, tm - 1)], POWER)
    left(halo, HALO)
    left(sup.at[pl.ds(0, boots - 1)], SUPPORT)
    left(outgoing.at[pl.ds(0, tm - 1)], SCATTER + ITERS - 1)
    left(gathered.at[pl.ds(0, tm - 1)], GATHER + ITERS - 2)
    left(norms.at[pl.ds(0, tm - 1)], NORMS)
    left(zx.at[pl.ds(0, boots - 1)], BOOTS)
    left(final.at[pl.ds(0, tm - 1)], FINAL)


def per_device(recording, starts, lengths, support):
    tm = lax.axis_size("tm")
    boots = lax.axis_size("boot")
    vmem = pl.BlockSpec(memory_space=pltpu.VMEM)
    anywhere = pl.BlockSpec(memory_space=pltpu.HBM)
    packed = pl.pallas_call(
        functools.partial(kernel, tm, boots),
        out_shape=jax.ShapeDtypeStruct((3 * RESP, SEG), jnp.float32),
        in_specs=[anywhere] * 4,
        out_specs=vmem,
        scratch_shapes=[
            pltpu.VMEM((SEG, CHANNELS), jnp.bfloat16),
            pltpu.SMEM((1, NBLK), jnp.int32),
            pltpu.SMEM((1, NBLK), jnp.int32),
            pltpu.VMEM((HEAD, CHANNELS), jnp.bfloat16),
            pltpu.VMEM((tm, 1, CHANNELS), jnp.float32),
            pltpu.VMEM((boots, boots, FEAT // boots), jnp.int32),
            pltpu.VMEM((WINDOW, CHANNELS), jnp.bfloat16),
            pltpu.VMEM((CAP, FEAT), jnp.bfloat16),
            pltpu.VMEM((RESP, FEAT), jnp.float32),
            pltpu.VMEM((RESP, FEAT), jnp.float32),
            pltpu.VMEM((RESP, FEAT), jnp.float32),
            pltpu.VMEM((RESP, FEAT), jnp.bfloat16),
            pltpu.VMEM((CAP, CAP), jnp.float32),
            pltpu.VMEM((tm, RESP, CHUNK), jnp.bfloat16),
            pltpu.VMEM((tm - 1, RESP, CHUNK), jnp.bfloat16),
            pltpu.VMEM((tm, RESP, CHUNK), jnp.bfloat16),
            pltpu.VMEM((tm, 1, CHUNK), jnp.float32),
            pltpu.VMEM((boots, RESP, CHUNK), jnp.bfloat16),
            pltpu.VMEM((tm, RESP, CHUNK), jnp.bfloat16),
            pltpu.SemaphoreType.DMA((PHASES,)),
            pltpu.SemaphoreType.DMA((PHASES,)),
            pltpu.SemaphoreType.DMA((4,)),
        ],
        compiler_params=pltpu.CompilerParams(
            collective_id=0, has_side_effects=True, vmem_limit_bytes=48 * 1024 * 1024
        ),
    )(*(pltpu.with_memory_space_constraint(a, pltpu.HBM) for a in (recording, starts, lengths, support)))
    return packed[2 * RESP :], packed[:RESP] - packed[RESP : 2 * RESP]


def solution(mesh):
    in_specs = (P("tm", None), P("boot", "tm"), P("boot", "tm"), P(None, "boot"))
    out_specs = (P(None, "boot"), P(None, "tm"))
    return jax.shard_map(
        per_device, mesh=mesh, in_specs=in_specs, out_specs=out_specs, check_vma=False
    )
```

```python
import functools

import jax
import jax.numpy as jnp
from jax import lax
from jax.experimental import pallas as pl
from jax.experimental.pallas import tpu as pltpu
from jax.sharding import PartitionSpec as P

CHANNELS = 1024
LAGS = 4
FEAT = LAGS * CHANNELS
RESP = 32
NBLK = 6
CAP = 384
SEG = 512
ITERS = 3
CHEB = 5
HEAD = 16
WINDOW = 640
CHUNK = 128

RHO = 4.0
SHRINK = 0.75
EPSILON = 1e-05

HIGHEST = lax.Precision.HIGHEST
NT = (((1,), (1,)), ((), ()))
NN = (((1,), (0,)), ((), ()))
HALO, POWER, SUPPORT, SCATTER, GATHER, NORMS, BOOTS, FINAL = 0, 1, 2, 3, 6, 8, 9, 10
PHASES = 11


def split(a):
    high = a.astype(jnp.bfloat16)
    return high, (a - high.astype(jnp.float32)).astype(jnp.bfloat16)


def times(a, high, low):
    rows = a.shape[0]
    first, rest = split(a)
    out = jnp.dot(
        jnp.concatenate([first, rest], axis=0), high, preferred_element_type=jnp.float32
    )
    return out[:rows] + (out[rows:] + jnp.dot(first, low, preferred_element_type=jnp.float32))


def chebyshev(gram, rhs, bound):
    high, low = split(gram)
    theta = RHO + 0.5 * bound
    delta = 0.5 * bound
    sigma = theta / delta
    total = jnp.zeros_like(rhs)
    remain = rhs
    factor = 1.0 / sigma
    update = rhs / theta
    for count in range(CHEB):
        total = total + update
        if count + 1 < CHEB:
            applied = RHO * update + times(update, high, low)
            remain = remain - applied
            after = 1.0 / (2.0 * sigma - factor)
            update = after * factor * update + 2.0 * after / delta * remain
            factor = after
    return total


def chebyshev_terms(bound):
    theta = RHO + 0.5 * bound
    delta = 0.5 * bound
    sigma = theta / delta
    nought = jnp.zeros_like(bound)
    total = [nought] * CHEB
    remain = [jnp.ones_like(bound)] + [nought] * (CHEB - 1)
    factor = 1.0 / sigma
    update = [term / theta for term in remain]
    for count in range(CHEB):
        total = [a + b for a, b in zip(total, update)]
        if count + 1 < CHEB:
            applied = [
                theta * update[k] + (delta * update[k - 1] if k else 0.0)
                for k in range(CHEB)
            ]
            remain = [a - b for a, b in zip(remain, applied)]
            after = 1.0 / (2.0 * sigma - factor)
            update = [
                after * factor * d + 2.0 * after / delta * r
                for d, r in zip(update, remain)
            ]
            factor = after
    return total, delta


def far_first():
    offsets = [(d, p, a, c) for d in range(4) for p in range(2) for a in range(2) for c in range(2)]
    hops = {o: min(o[0], 4 - o[0]) + (2 if o[1] > o[2] else o[1] | o[2]) for o in offsets}
    return sorted(offsets[1:], key=lambda o: -hops[o])


def kernel(
    tm,
    boots,
    rec_hbm,
    starts_hbm,
    lengths_hbm,
    support_hbm,
    packed,
    rec,
    starts_ref,
    lengths_ref,
    halo,
    power,
    sup,
    ext,
    design,
    turned,
    cross,
    v,
    z,
    solver,
    solver_high,
    solver_low,
    outgoing,
    incoming,
    gathered,
    norms,
    zx,
    final,
    send_sem,
    recv_sem,
    local_sem,
):
    b = lax.axis_index("boot")
    me = lax.axis_index("tm")
    x, y, core = me // 8, lax.rem(me // 2, 4), lax.rem(me, 2)
    offsets = far_first()

    def tm_at(o):
        pair, place = lax.rem(y // 2 + o[1], 2), lax.rem(lax.rem(y, 2) + o[2], 2)
        return lax.rem(x + o[0], 4) * 8 + pair * 4 + place * 2 + lax.rem(core + o[3], 2)

    def tm_peer(i):
        return lax.rem(me + i, tm)

    def boot_peer(i):
        return lax.rem(b + i, boots)

    barrier = pltpu.get_barrier_semaphore()

    @pl.loop(1, tm)
    def _(i):
        pl.semaphore_signal(
            barrier, inc=1, device_id={"tm": tm_peer(i)}, device_id_type=pl.DeviceIdType.MESH
        )

    @pl.loop(1, boots)
    def _(i):
        pl.semaphore_signal(
            barrier, inc=1, device_id={"boot": boot_peer(i)}, device_id_type=pl.DeviceIdType.MESH
        )

    def fetch(src, dst, k):
        copy = pltpu.make_async_copy(src, dst, local_sem.at[k])
        copy.start()
        return copy

    rec_copy = fetch(rec_hbm, rec, 0)
    starts_copy = fetch(starts_hbm, starts_ref, 1)
    lengths_copy = fetch(lengths_hbm, lengths_ref, 2)
    support_copy = fetch(support_hbm, sup.at[b], 3)

    def send(src, dst, phase, target):
        pltpu.make_async_remote_copy(
            src_ref=src,
            dst_ref=dst,
            send_sem=send_sem.at[phase],
            recv_sem=recv_sem.at[phase],
            device_id=target,
            device_id_type=pl.DeviceIdType.MESH,
        ).start()

    def to_tm(src, dst, phase):
        for o in offsets:
            send(src, dst, phase, {"tm": tm_at(o)})

    def to_boots(src, dst, phase):
        for i in (4, 3, 5, 2, 6, 1, 7):
            send(src, dst, phase, {"boot": boot_peer(i)})

    def arrived(ref, phase):
        pltpu.make_async_copy(ref, ref, recv_sem.at[phase]).wait()

    def left(ref, phase):
        pltpu.make_async_copy(ref, ref, send_sem.at[phase]).wait()

    rec_copy.wait()
    acc = jnp.zeros((8, CHANNELS), jnp.float32)

    def add_rows(k, acc):
        block = rec[pl.ds(pl.multiple_of(k * 16, 16), 16), :].astype(jnp.float32)
        block = block * block
        return acc + block[:8] + block[8:]

    acc = lax.fori_loop(0, SEG // 16, add_rows, acc)
    power[me] = jnp.sum(acc, axis=0, keepdims=True)

    starts_copy.wait()
    lengths_copy.wait()
    row = lax.broadcasted_iota(jnp.int32, (CAP, CHUNK), 0)
    place = jnp.full((CAP, CHUNK), -4 * SEG, jnp.int32)
    offset = jnp.int32(0)
    for k in range(NBLK):
        length = lengths_ref[0, k]
        inside = (row >= offset) & (row < offset + length)
        place = jnp.where(inside, row + (starts_ref[0, k] - offset), place)
        offset = offset + length
    lane = lax.broadcasted_iota(jnp.int32, (CAP, CHUNK), 1)

    def picks(back, width):
        return jnp.concatenate(
            [
                jnp.where(place - back == lane + c * CHUNK, 1.0, 0.0).astype(jnp.bfloat16)
                for c in range(width // CHUNK)
            ],
            axis=1,
        )

    def raw_rows(lag):
        pick = picks(1 + lag, SEG)
        for part in range(4):
            at = lag * CHANNELS + part * 256
            design[:, at : at + 256] = jnp.dot(
                pick, rec[:, part * 256 : (part + 1) * 256], preferred_element_type=jnp.float32
            ).astype(jnp.bfloat16)

    support_copy.wait()
    raw_rows(0)
    pl.semaphore_wait(barrier, tm + boots - 2)
    send(rec_hbm.at[pl.ds(SEG - HEAD, HEAD)], halo, HALO, {"tm": tm_peer(1)})
    to_tm(power.at[me], power.at[me], POWER)
    to_boots(support_hbm, sup.at[b], SUPPORT)
    raw_rows(1)
    raw_rows(2)
    raw_rows(3)
    answer = jnp.dot(picks(0, SEG), rec[:, :CHUNK], preferred_element_type=jnp.float32)
    arrived(halo, HALO)
    before = halo[...]
    before = jnp.where(me == 0, jnp.zeros_like(before), before)
    behind = lane - HEAD
    for lag in range(LAGS):
        cols = slice(lag * CHANNELS, (lag + 1) * CHANNELS)
        reach = jnp.where(place - 1 - lag == behind, 1.0, 0.0).astype(jnp.bfloat16)[:, :HEAD]
        extra = jnp.dot(reach, before, preferred_element_type=jnp.float32)
        design[:, cols] = (design[:, cols].astype(jnp.float32) + extra).astype(jnp.bfloat16)
    arrived(power.at[pl.ds(0, tm - 1)], POWER)
    total = jnp.sum(power[...], axis=0)
    scale = 1.0 / jnp.sqrt(total / (SEG * tm) + EPSILON)

    answer = (answer * scale[:, :CHUNK]).astype(jnp.bfloat16).astype(jnp.float32)
    answer = jnp.transpose(answer)[:RESP].astype(jnp.bfloat16)
    gram = jnp.zeros((CAP, CAP), jnp.float32)
    projected = jnp.zeros((RESP, CAP), jnp.float32)
    for lag in range(LAGS):
        cols = slice(lag * CHANNELS, (lag + 1) * CHANNELS)
        piece = (design[:, cols].astype(jnp.float32) * scale).astype(jnp.bfloat16)
        design[:, cols] = piece
        gram = gram + lax.dot_general(piece, piece, NT, preferred_element_type=jnp.float32)
        fit = jnp.dot(answer, piece, preferred_element_type=jnp.float32) * (1.0 / CAP)
        cross[:, cols] = fit
        projected = projected + lax.dot_general(
            fit.astype(jnp.bfloat16), piece, NT, preferred_element_type=jnp.float32
        )
    gram = gram * (1.0 / CAP)
    solver[...] = gram
    bound = jnp.sqrt(jnp.sum(jnp.sum(gram * gram, axis=1, keepdims=True), axis=0, keepdims=True))

    def flip(lag):
        cols = slice(lag * CHANNELS, (lag + 1) * CHANNELS)
        turned[cols, :] = jnp.transpose(design[:, cols])

    mine = pl.ds(pl.multiple_of(me * CHUNK, CHUNK), CHUNK)
    for it in range(ITERS):
        projected = projected * (1.0 / CAP)
        if it == 0:
            weights = chebyshev(solver[...], projected, bound)
        else:
            weights = times(projected, solver_high[...], solver_low[...])
        weights = weights.astype(jnp.bfloat16)
        if it:
            left(outgoing.at[pl.ds(0, tm - 1)], SCATTER + it - 1)
        for dx, dp in ((2, 1), (2, 0), (1, 1), (3, 1), (1, 0), (3, 0), (0, 1), (0, 0)):
            group = lax.rem(x + dx, 4) * 2 + lax.rem(y // 2 + dp, 2)
            cols = pl.ds(pl.multiple_of(group * 512, 512), 512)
            back = jnp.dot(weights, design[:, cols], preferred_element_type=jnp.float32)
            value = (cross[:, cols] - back) * (1.0 / RHO)
            v[:, cols] = value
            for c in range(4):
                outgoing[group * 4 + c] = value[:, c * CHUNK : (c + 1) * CHUNK].astype(jnp.bfloat16)
            for slot, o in enumerate(offsets):
                if o[:2] == (dx, dp):
                    peer = tm_at(o)
                    send(outgoing.at[peer], incoming.at[slot], SCATTER + it, {"tm": peer})

        if it == 0:
            terms, delta = chebyshev_terms(bound)
            ri = lax.broadcasted_iota(jnp.int32, (CAP, CAP), 0)
            ci = lax.broadcasted_iota(jnp.int32, (CAP, CAP), 1)
            eye = jnp.where(ri == ci, 1.0, 0.0)
            x1 = solver[...] * (1.0 / delta) - eye
            x2 = jnp.dot(x1, x1, precision=HIGHEST, preferred_element_type=jnp.float32)
            solver_high[...], solver_low[...] = split(
                terms[0] * eye
                + terms[1] * x1
                + terms[2] * x2
                + jnp.dot(
                    x2,
                    terms[3] * x1 + terms[4] * x2,
                    precision=HIGHEST,
                    preferred_element_type=jnp.float32,
                )
            )

            flip(0)

        arrived(incoming, SCATTER + it)
        mean = v[:, mine]
        for i in range(tm - 1):
            mean = mean + incoming[i].astype(jnp.float32)
        mean = mean * (1.0 / tm)
        if it:
            mean = mean + z[:, mine]
        if it + 1 < ITERS:
            if it:
                left(gathered.at[pl.ds(0, tm - 1)], GATHER + it - 1)
            gathered[me] = mean.astype(jnp.bfloat16)
            to_tm(gathered.at[me], gathered.at[me], GATHER + it)
            if it == 0:
                flip(1)
                flip(2)
                flip(3)
            else:
                def scale_rows(k, carry):
                    at = pl.multiple_of(k * 16, 16)
                    block = rec[pl.ds(at, 16), :].astype(jnp.float32) * scale
                    ext[pl.ds(pl.multiple_of(at + HEAD, 16), 16), :] = block.astype(jnp.bfloat16)
                    return carry

                lax.fori_loop(0, SEG // 16, scale_rows, 0)
                ext[0:HEAD, :] = (before.astype(jnp.float32) * scale).astype(jnp.bfloat16)
                ext[HEAD + SEG :, :] = jnp.zeros((WINDOW - HEAD - SEG, CHANNELS), jnp.bfloat16)
                normed = ext[HEAD : HEAD + SEG, :CHUNK].astype(jnp.float32)
                packed[:RESP] = jnp.transpose(normed)[:RESP]
            arrived(gathered.at[pl.ds(0, tm - 1)], GATHER + it)
            lengths = []
            for c in range(tm):
                block = gathered[c].astype(jnp.float32)
                lengths.append(jnp.sqrt(jnp.sum(block * block, axis=0, keepdims=True)))
            level = (
                jnp.sum(functools.reduce(jnp.add, lengths), axis=1, keepdims=True)
                * (SHRINK / FEAT)
            )
            projected = jnp.zeros((RESP, CAP), jnp.float32)
            for part in range(8):
                targets = []
                for c in range(part * 4, part * 4 + 4):
                    cols = slice(c * CHUNK, (c + 1) * CHUNK)
                    factor = jnp.maximum(lengths[c] - level, 0.0) / jnp.maximum(lengths[c], level)
                    fresh = gathered[c].astype(jnp.float32) * factor
                    dual = v[:, cols] - fresh
                    if it:
                        dual = dual + z[:, cols]
                    z[:, cols] = fresh
                    targets.append((cross[:, cols] + RHO * (fresh - dual)).astype(jnp.bfloat16))
                projected = projected + lax.dot_general(
                    jnp.concatenate(targets, axis=1),
                    turned[part * 512 : (part + 1) * 512, :],
                    NN,
                    preferred_element_type=jnp.float32,
                )
    length = jnp.sqrt(jnp.sum(mean * mean, axis=0, keepdims=True))
    norms[me] = length
    to_tm(norms.at[me], norms.at[me], NORMS)
    arrived(norms.at[pl.ds(0, tm - 1)], NORMS)
    level = jnp.sum(jnp.sum(norms[...], axis=0), axis=1, keepdims=True) * (SHRINK / FEAT)
    factor = jnp.maximum(length - level, 0.0) / jnp.maximum(length, level)
    zx[b] = (mean * factor).astype(jnp.bfloat16)
    to_boots(zx.at[b], zx.at[b], BOOTS)
    arrived(sup.at[pl.ds(0, boots - 1)], SUPPORT)
    quarter = pl.ds(pl.multiple_of(lax.rem(me, 4) * CHUNK, CHUNK), CHUNK)
    chosen = sup[me // 4, :, quarter].astype(jnp.float32)
    tally = jnp.maximum(jnp.sum(chosen, axis=0, keepdims=True), 1.0)
    arrived(zx.at[pl.ds(0, boots - 1)], BOOTS)
    average = jnp.zeros((RESP, CHUNK), jnp.float32)
    for k in range(boots):
        average = average + chosen[k : k + 1] * zx[k].astype(jnp.float32)
    average = average / tally
    final[me] = average.astype(jnp.bfloat16)
    to_tm(final.at[me], final.at[me], FINAL)
    arrived(final.at[pl.ds(0, tm - 1)], FINAL)
    for c in range(4):
        packed[2 * RESP :, c * CHUNK : (c + 1) * CHUNK] = final[4 * b + c].astype(jnp.float32)
    stacked = jnp.concatenate(
        [
            jnp.concatenate([final[lag * 8 + c] for c in range(8)], axis=1)
            for lag in range(LAGS)
        ],
        axis=0,
    )
    forecast = lax.dot_general(stacked, ext[...], NT, preferred_element_type=jnp.float32)
    told = jnp.zeros((RESP, SEG), jnp.float32)
    for lag in range(LAGS):
        begin = HEAD - 1 - lag
        shifted = pltpu.roll(forecast[lag * RESP : (lag + 1) * RESP], WINDOW - begin, 1)
        told = told + shifted[:, :SEG]
    packed[RESP : 2 * RESP] = told

    left(power.at[pl.ds(0, tm - 1)], POWER)
    left(halo, HALO)
    left(sup.at[pl.ds(0, boots - 1)], SUPPORT)
    left(outgoing.at[pl.ds(0, tm - 1)], SCATTER + ITERS - 1)
    left(gathered.at[pl.ds(0, tm - 1)], GATHER + ITERS - 2)
    left(norms.at[pl.ds(0, tm - 1)], NORMS)
    left(zx.at[pl.ds(0, boots - 1)], BOOTS)
    left(final.at[pl.ds(0, tm - 1)], FINAL)


def per_device(recording, starts, lengths, support):
    tm = lax.axis_size("tm")
    boots = lax.axis_size("boot")
    vmem = pl.BlockSpec(memory_space=pltpu.VMEM)
    anywhere = pl.BlockSpec(memory_space=pltpu.HBM)
    packed = pl.pallas_call(
        functools.partial(kernel, tm, boots),
        out_shape=jax.ShapeDtypeStruct((3 * RESP, SEG), jnp.float32),
        in_specs=[anywhere] * 4,
        out_specs=vmem,
        scratch_shapes=[
            pltpu.VMEM((SEG, CHANNELS), jnp.bfloat16),
            pltpu.SMEM((1, NBLK), jnp.int32),
            pltpu.SMEM((1, NBLK), jnp.int32),
            pltpu.VMEM((HEAD, CHANNELS), jnp.bfloat16),
            pltpu.VMEM((tm, 1, CHANNELS), jnp.float32),
            pltpu.VMEM((boots, boots, FEAT // boots), jnp.int32),
            pltpu.VMEM((WINDOW, CHANNELS), jnp.bfloat16),
            pltpu.VMEM((CAP, FEAT), jnp.bfloat16),
            pltpu.VMEM((FEAT, CAP), jnp.bfloat16),
            pltpu.VMEM((RESP, FEAT), jnp.float32),
            pltpu.VMEM((RESP, FEAT), jnp.float32),
            pltpu.VMEM((RESP, FEAT), jnp.float32),
            pltpu.VMEM((CAP, CAP), jnp.float32),
            pltpu.VMEM((CAP, CAP), jnp.bfloat16),
            pltpu.VMEM((CAP, CAP), jnp.bfloat16),
            pltpu.VMEM((tm, RESP, CHUNK), jnp.bfloat16),
            pltpu.VMEM((tm - 1, RESP, CHUNK), jnp.bfloat16),
            pltpu.VMEM((tm, RESP, CHUNK), jnp.bfloat16),
            pltpu.VMEM((tm, 1, CHUNK), jnp.float32),
            pltpu.VMEM((boots, RESP, CHUNK), jnp.bfloat16),
            pltpu.VMEM((tm, RESP, CHUNK), jnp.bfloat16),
            pltpu.SemaphoreType.DMA((PHASES,)),
            pltpu.SemaphoreType.DMA((PHASES,)),
            pltpu.SemaphoreType.DMA((4,)),
        ],
        compiler_params=pltpu.CompilerParams(
            collective_id=0, has_side_effects=True, vmem_limit_bytes=48 * 1024 * 1024
        ),
    )(*(pltpu.with_memory_space_constraint(a, pltpu.HBM) for a in (recording, starts, lengths, support)))
    return packed[2 * RESP :], packed[:RESP] - packed[RESP : 2 * RESP]


def solution(mesh):
    in_specs = (P("tm", None), P("boot", "tm"), P("boot", "tm"), P(None, "boot"))
    out_specs = (P(None, "boot"), P(None, "tm"))
    return jax.shard_map(
        per_device, mesh=mesh, in_specs=in_specs, out_specs=out_specs, check_vma=False
    )
```

```python
import functools

import jax
import jax.numpy as jnp
from jax import lax
from jax.experimental import pallas as pl
from jax.experimental.pallas import tpu as pltpu
from jax.sharding import PartitionSpec as P

CHANNELS = 1024
LAGS = 4
FEAT = LAGS * CHANNELS
RESP = 32
NBLK = 6
CAP = 384
SEG = 512
ITERS = 3
CHEB = 5
HEAD = 16
WINDOW = 640
CHUNK = 128

RHO = 4.0
SHRINK = 0.75
EPSILON = 1e-05

HIGHEST = lax.Precision.HIGHEST
NT = (((1,), (1,)), ((), ()))
NN = (((1,), (0,)), ((), ()))
HALO, POWER, SUPPORT, SCATTER, GATHER, NORMS, BOOTS, FINAL = 0, 1, 2, 3, 6, 8, 9, 10
PHASES = 11


def split(a):
    high = a.astype(jnp.bfloat16)
    return high, (a - high.astype(jnp.float32)).astype(jnp.bfloat16)


def times(a, high, low):
    rows = a.shape[0]
    first, rest = split(a)
    out = jnp.dot(
        jnp.concatenate([first, rest], axis=0), high, preferred_element_type=jnp.float32
    )
    return out[:rows] + (out[rows:] + jnp.dot(first, low, preferred_element_type=jnp.float32))


def chebyshev(gram, rhs, bound):
    high, low = split(gram)
    theta = RHO + 0.5 * bound
    delta = 0.5 * bound
    sigma = theta / delta
    total = jnp.zeros_like(rhs)
    remain = rhs
    factor = 1.0 / sigma
    update = rhs / theta
    for count in range(CHEB):
        total = total + update
        if count + 1 < CHEB:
            applied = RHO * update + times(update, high, low)
            remain = remain - applied
            after = 1.0 / (2.0 * sigma - factor)
            update = after * factor * update + 2.0 * after / delta * remain
            factor = after
    return total


def chebyshev_terms(bound):
    theta = RHO + 0.5 * bound
    delta = 0.5 * bound
    sigma = theta / delta
    nought = jnp.zeros_like(bound)
    total = [nought] * CHEB
    remain = [jnp.ones_like(bound)] + [nought] * (CHEB - 1)
    factor = 1.0 / sigma
    update = [term / theta for term in remain]
    for count in range(CHEB):
        total = [a + b for a, b in zip(total, update)]
        if count + 1 < CHEB:
            applied = [
                theta * update[k] + (delta * update[k - 1] if k else 0.0)
                for k in range(CHEB)
            ]
            remain = [a - b for a, b in zip(remain, applied)]
            after = 1.0 / (2.0 * sigma - factor)
            update = [
                after * factor * d + 2.0 * after / delta * r
                for d, r in zip(update, remain)
            ]
            factor = after
    return total, delta


def far_first():
    offsets = [(d, p, a, c) for d in range(4) for p in range(2) for a in range(2) for c in range(2)]
    hops = {o: min(o[0], 4 - o[0]) + (2 if o[1] > o[2] else o[1] | o[2]) for o in offsets}
    return sorted(offsets[1:], key=lambda o: -hops[o])


def kernel(
    tm,
    boots,
    rec_hbm,
    starts_hbm,
    lengths_hbm,
    support_hbm,
    packed,
    rec,
    starts_ref,
    lengths_ref,
    halo,
    power,
    sup,
    ext,
    design,
    turned,
    cross,
    v,
    z,
    solver,
    solver_high,
    solver_low,
    outgoing,
    incoming,
    gathered,
    norms,
    zx,
    final,
    send_sem,
    recv_sem,
    local_sem,
):
    b = lax.axis_index("boot")
    me = lax.axis_index("tm")
    x, y, core = me // 8, lax.rem(me // 2, 4), lax.rem(me, 2)
    offsets = far_first()

    def tm_at(o):
        pair, place = lax.rem(y // 2 + o[1], 2), lax.rem(lax.rem(y, 2) + o[2], 2)
        return lax.rem(x + o[0], 4) * 8 + pair * 4 + place * 2 + lax.rem(core + o[3], 2)

    def tm_peer(i):
        return lax.rem(me + i, tm)

    def boot_peer(i):
        return lax.rem(b + i, boots)

    barrier = pltpu.get_barrier_semaphore()

    @pl.loop(1, tm)
    def _(i):
        pl.semaphore_signal(
            barrier, inc=1, device_id={"tm": tm_peer(i)}, device_id_type=pl.DeviceIdType.MESH
        )

    @pl.loop(1, boots)
    def _(i):
        pl.semaphore_signal(
            barrier, inc=1, device_id={"boot": boot_peer(i)}, device_id_type=pl.DeviceIdType.MESH
        )

    def fetch(src, dst, k):
        copy = pltpu.make_async_copy(src, dst, local_sem.at[k])
        copy.start()
        return copy

    rec_copy = fetch(rec_hbm, rec, 0)
    starts_copy = fetch(starts_hbm, starts_ref, 1)
    lengths_copy = fetch(lengths_hbm, lengths_ref, 2)
    support_copy = fetch(support_hbm, sup.at[b], 3)

    def send(src, dst, phase, target):
        pltpu.make_async_remote_copy(
            src_ref=src,
            dst_ref=dst,
            send_sem=send_sem.at[phase],
            recv_sem=recv_sem.at[phase],
            device_id=target,
            device_id_type=pl.DeviceIdType.MESH,
        ).start()

    def to_tm(src, dst, phase):
        for o in offsets:
            send(src, dst, phase, {"tm": tm_at(o)})

    def to_boots(src, dst, phase):
        for i in (4, 3, 5, 2, 6, 1, 7):
            send(src, dst, phase, {"boot": boot_peer(i)})

    def arrived(ref, phase):
        pltpu.make_async_copy(ref, ref, recv_sem.at[phase]).wait()

    def left(ref, phase):
        pltpu.make_async_copy(ref, ref, send_sem.at[phase]).wait()

    rec_copy.wait()
    acc = jnp.zeros((8, CHANNELS), jnp.float32)

    def add_rows(k, acc):
        block = rec[pl.ds(pl.multiple_of(k * 16, 16), 16), :].astype(jnp.float32)
        block = block * block
        return acc + block[:8] + block[8:]

    acc = lax.fori_loop(0, SEG // 16, add_rows, acc)
    power[me] = jnp.sum(acc, axis=0, keepdims=True)

    starts_copy.wait()
    lengths_copy.wait()
    row = lax.broadcasted_iota(jnp.int32, (CAP, CHUNK), 0)
    place = jnp.full((CAP, CHUNK), -4 * SEG, jnp.int32)
    offset = jnp.int32(0)
    for k in range(NBLK):
        length = lengths_ref[0, k]
        inside = (row >= offset) & (row < offset + length)
        place = jnp.where(inside, row + (starts_ref[0, k] - offset), place)
        offset = offset + length
    lane = lax.broadcasted_iota(jnp.int32, (CAP, CHUNK), 1)

    def picks(back, width):
        return jnp.concatenate(
            [
                jnp.where(place - back == lane + c * CHUNK, 1.0, 0.0).astype(jnp.bfloat16)
                for c in range(width // CHUNK)
            ],
            axis=1,
        )

    def raw_rows(lag):
        pick = picks(1 + lag, SEG)
        for part in range(4):
            at = lag * CHANNELS + part * 256
            design[:, at : at + 256] = jnp.dot(
                pick, rec[:, part * 256 : (part + 1) * 256], preferred_element_type=jnp.float32
            ).astype(jnp.bfloat16)

    support_copy.wait()
    raw_rows(0)
    pl.semaphore_wait(barrier, tm + boots - 2)
    send(rec_hbm.at[pl.ds(SEG - HEAD, HEAD)], halo, HALO, {"tm": tm_peer(1)})
    to_tm(power.at[me], power.at[me], POWER)
    to_boots(support_hbm, sup.at[b], SUPPORT)
    raw_rows(1)
    raw_rows(2)
    raw_rows(3)
    answer = jnp.dot(picks(0, SEG), rec[:, :CHUNK], preferred_element_type=jnp.float32)
    arrived(halo, HALO)
    before = halo[...]
    before = jnp.where(me == 0, jnp.zeros_like(before), before)
    behind = lane - HEAD
    for lag in range(LAGS):
        cols = slice(lag * CHANNELS, (lag + 1) * CHANNELS)
        reach = jnp.where(place - 1 - lag == behind, 1.0, 0.0).astype(jnp.bfloat16)[:, :HEAD]
        extra = jnp.dot(reach, before, preferred_element_type=jnp.float32)
        design[:, cols] = (design[:, cols].astype(jnp.float32) + extra).astype(jnp.bfloat16)
    arrived(power.at[pl.ds(0, tm - 1)], POWER)
    total = jnp.sum(power[...], axis=0)
    scale = 1.0 / jnp.sqrt(total / (SEG * tm) + EPSILON)

    answer = (answer * scale[:, :CHUNK]).astype(jnp.bfloat16).astype(jnp.float32)
    answer = jnp.transpose(answer)[:RESP].astype(jnp.bfloat16)
    both = jnp.zeros((CAP + RESP, CAP), jnp.float32)
    for lag in range(LAGS):
        cols = slice(lag * CHANNELS, (lag + 1) * CHANNELS)
        piece = (design[:, cols].astype(jnp.float32) * scale).astype(jnp.bfloat16)
        design[:, cols] = piece
        fit = jnp.dot(answer, piece, preferred_element_type=jnp.float32) * (1.0 / CAP)
        cross[:, cols] = fit
        both = both + lax.dot_general(
            jnp.concatenate([piece, fit.astype(jnp.bfloat16)], axis=0),
            piece,
            NT,
            preferred_element_type=jnp.float32,
        )
    gram = both[:CAP] * (1.0 / CAP)
    projected = both[CAP:]
    solver[...] = gram
    bound = jnp.sqrt(jnp.sum(jnp.sum(gram * gram, axis=1, keepdims=True), axis=0, keepdims=True))

    def flip(lag):
        cols = slice(lag * CHANNELS, (lag + 1) * CHANNELS)
        turned[cols, :] = jnp.transpose(design[:, cols])

    mine = pl.ds(pl.multiple_of(me * CHUNK, CHUNK), CHUNK)
    for it in range(ITERS):
        projected = projected * (1.0 / CAP)
        if it == 0:
            weights = chebyshev(solver[...], projected, bound)
        else:
            weights = times(projected, solver_high[...], solver_low[...])
        weights = weights.astype(jnp.bfloat16)
        if it:
            left(outgoing.at[pl.ds(0, tm - 1)], SCATTER + it - 1)
        for dx, dp in ((2, 1), (2, 0), (1, 1), (3, 1), (1, 0), (3, 0), (0, 1), (0, 0)):
            group = lax.rem(x + dx, 4) * 2 + lax.rem(y // 2 + dp, 2)
            cols = pl.ds(pl.multiple_of(group * 512, 512), 512)
            back = jnp.dot(weights, design[:, cols], preferred_element_type=jnp.float32)
            value = (cross[:, cols] - back) * (1.0 / RHO)
            v[:, cols] = value
            for c in range(4):
                outgoing[group * 4 + c] = value[:, c * CHUNK : (c + 1) * CHUNK].astype(jnp.bfloat16)
            for slot, o in enumerate(offsets):
                if o[:2] == (dx, dp):
                    peer = tm_at(o)
                    send(outgoing.at[peer], incoming.at[slot], SCATTER + it, {"tm": peer})

        if it == 0:
            terms, delta = chebyshev_terms(bound)
            ri = lax.broadcasted_iota(jnp.int32, (CAP, CAP), 0)
            ci = lax.broadcasted_iota(jnp.int32, (CAP, CAP), 1)
            eye = jnp.where(ri == ci, 1.0, 0.0)
            x1 = solver[...] * (1.0 / delta) - eye
            x2 = jnp.dot(x1, x1, precision=HIGHEST, preferred_element_type=jnp.float32)
            solver_high[...], solver_low[...] = split(
                terms[0] * eye
                + terms[1] * x1
                + terms[2] * x2
                + jnp.dot(
                    x2,
                    terms[3] * x1 + terms[4] * x2,
                    precision=HIGHEST,
                    preferred_element_type=jnp.float32,
                )
            )

            flip(0)

        arrived(incoming, SCATTER + it)
        mean = v[:, mine]
        for i in range(tm - 1):
            mean = mean + incoming[i].astype(jnp.float32)
        mean = mean * (1.0 / tm)
        if it:
            mean = mean + z[:, mine]
        if it + 1 < ITERS:
            if it:
                left(gathered.at[pl.ds(0, tm - 1)], GATHER + it - 1)
            gathered[me] = mean.astype(jnp.bfloat16)
            to_tm(gathered.at[me], gathered.at[me], GATHER + it)
            if it == 0:
                flip(1)
                flip(2)
                flip(3)
            else:
                def scale_rows(k, carry):
                    at = pl.multiple_of(k * 16, 16)
                    block = rec[pl.ds(at, 16), :].astype(jnp.float32) * scale
                    ext[pl.ds(pl.multiple_of(at + HEAD, 16), 16), :] = block.astype(jnp.bfloat16)
                    return carry

                lax.fori_loop(0, SEG // 16, scale_rows, 0)
                ext[0:HEAD, :] = (before.astype(jnp.float32) * scale).astype(jnp.bfloat16)
                ext[HEAD + SEG :, :] = jnp.zeros((WINDOW - HEAD - SEG, CHANNELS), jnp.bfloat16)
                normed = ext[HEAD : HEAD + SEG, :CHUNK].astype(jnp.float32)
                packed[:RESP] = jnp.transpose(normed)[:RESP]
            arrived(gathered.at[pl.ds(0, tm - 1)], GATHER + it)
            lengths = []
            for c in range(tm):
                block = gathered[c].astype(jnp.float32)
                lengths.append(jnp.sqrt(jnp.sum(block * block, axis=0, keepdims=True)))
            level = (
                jnp.sum(functools.reduce(jnp.add, lengths), axis=1, keepdims=True)
                * (SHRINK / FEAT)
            )
            projected = jnp.zeros((RESP, CAP), jnp.float32)
            for part in range(8):
                targets = []
                for c in range(part * 4, part * 4 + 4):
                    cols = slice(c * CHUNK, (c + 1) * CHUNK)
                    factor = jnp.maximum(lengths[c] - level, 0.0) / jnp.maximum(lengths[c], level)
                    fresh = gathered[c].astype(jnp.float32) * factor
                    dual = v[:, cols] - fresh
                    if it:
                        dual = dual + z[:, cols]
                    z[:, cols] = fresh
                    targets.append((cross[:, cols] + RHO * (fresh - dual)).astype(jnp.bfloat16))
                projected = projected + lax.dot_general(
                    jnp.concatenate(targets, axis=1),
                    turned[part * 512 : (part + 1) * 512, :],
                    NN,
                    preferred_element_type=jnp.float32,
                )
    length = jnp.sqrt(jnp.sum(mean * mean, axis=0, keepdims=True))
    norms[me] = length
    to_tm(norms.at[me], norms.at[me], NORMS)
    arrived(norms.at[pl.ds(0, tm - 1)], NORMS)
    level = jnp.sum(jnp.sum(norms[...], axis=0), axis=1, keepdims=True) * (SHRINK / FEAT)
    factor = jnp.maximum(length - level, 0.0) / jnp.maximum(length, level)
    zx[b] = (mean * factor).astype(jnp.bfloat16)
    to_boots(zx.at[b], zx.at[b], BOOTS)
    arrived(sup.at[pl.ds(0, boots - 1)], SUPPORT)
    quarter = pl.ds(pl.multiple_of(lax.rem(me, 4) * CHUNK, CHUNK), CHUNK)
    chosen = sup[me // 4, :, quarter].astype(jnp.float32)
    tally = jnp.maximum(jnp.sum(chosen, axis=0, keepdims=True), 1.0)
    arrived(zx.at[pl.ds(0, boots - 1)], BOOTS)
    average = jnp.zeros((RESP, CHUNK), jnp.float32)
    for k in range(boots):
        average = average + chosen[k : k + 1] * zx[k].astype(jnp.float32)
    average = average / tally
    final[me] = average.astype(jnp.bfloat16)
    to_tm(final.at[me], final.at[me], FINAL)
    arrived(final.at[pl.ds(0, tm - 1)], FINAL)
    for c in range(4):
        packed[2 * RESP :, c * CHUNK : (c + 1) * CHUNK] = final[4 * b + c].astype(jnp.float32)
    stacked = jnp.concatenate(
        [
            jnp.concatenate([final[lag * 8 + c] for c in range(8)], axis=1)
            for lag in range(LAGS)
        ],
        axis=0,
    )
    forecast = lax.dot_general(stacked, ext[...], NT, preferred_element_type=jnp.float32)
    told = jnp.zeros((RESP, SEG), jnp.float32)
    for lag in range(LAGS):
        begin = HEAD - 1 - lag
        shifted = pltpu.roll(forecast[lag * RESP : (lag + 1) * RESP], WINDOW - begin, 1)
        told = told + shifted[:, :SEG]
    packed[RESP : 2 * RESP] = told

    left(power.at[pl.ds(0, tm - 1)], POWER)
    left(halo, HALO)
    left(sup.at[pl.ds(0, boots - 1)], SUPPORT)
    left(outgoing.at[pl.ds(0, tm - 1)], SCATTER + ITERS - 1)
    left(gathered.at[pl.ds(0, tm - 1)], GATHER + ITERS - 2)
    left(norms.at[pl.ds(0, tm - 1)], NORMS)
    left(zx.at[pl.ds(0, boots - 1)], BOOTS)
    left(final.at[pl.ds(0, tm - 1)], FINAL)


def per_device(recording, starts, lengths, support):
    tm = lax.axis_size("tm")
    boots = lax.axis_size("boot")
    vmem = pl.BlockSpec(memory_space=pltpu.VMEM)
    anywhere = pl.BlockSpec(memory_space=pltpu.HBM)
    packed = pl.pallas_call(
        functools.partial(kernel, tm, boots),
        out_shape=jax.ShapeDtypeStruct((3 * RESP, SEG), jnp.float32),
        in_specs=[anywhere] * 4,
        out_specs=vmem,
        scratch_shapes=[
            pltpu.VMEM((SEG, CHANNELS), jnp.bfloat16),
            pltpu.SMEM((1, NBLK), jnp.int32),
            pltpu.SMEM((1, NBLK), jnp.int32),
            pltpu.VMEM((HEAD, CHANNELS), jnp.bfloat16),
            pltpu.VMEM((tm, 1, CHANNELS), jnp.float32),
            pltpu.VMEM((boots, boots, FEAT // boots), jnp.int32),
            pltpu.VMEM((WINDOW, CHANNELS), jnp.bfloat16),
            pltpu.VMEM((CAP, FEAT), jnp.bfloat16),
            pltpu.VMEM((FEAT, CAP), jnp.bfloat16),
            pltpu.VMEM((RESP, FEAT), jnp.float32),
            pltpu.VMEM((RESP, FEAT), jnp.float32),
            pltpu.VMEM((RESP, FEAT), jnp.float32),
            pltpu.VMEM((CAP, CAP), jnp.float32),
            pltpu.VMEM((CAP, CAP), jnp.bfloat16),
            pltpu.VMEM((CAP, CAP), jnp.bfloat16),
            pltpu.VMEM((tm, RESP, CHUNK), jnp.bfloat16),
            pltpu.VMEM((tm - 1, RESP, CHUNK), jnp.bfloat16),
            pltpu.VMEM((tm, RESP, CHUNK), jnp.bfloat16),
            pltpu.VMEM((tm, 1, CHUNK), jnp.float32),
            pltpu.VMEM((boots, RESP, CHUNK), jnp.bfloat16),
            pltpu.VMEM((tm, RESP, CHUNK), jnp.bfloat16),
            pltpu.SemaphoreType.DMA((PHASES,)),
            pltpu.SemaphoreType.DMA((PHASES,)),
            pltpu.SemaphoreType.DMA((4,)),
        ],
        compiler_params=pltpu.CompilerParams(
            collective_id=0, has_side_effects=True, vmem_limit_bytes=48 * 1024 * 1024
        ),
    )(*(pltpu.with_memory_space_constraint(a, pltpu.HBM) for a in (recording, starts, lengths, support)))
    return packed[2 * RESP :], packed[:RESP] - packed[RESP : 2 * RESP]


def solution(mesh):
    in_specs = (P("tm", None), P("boot", "tm"), P("boot", "tm"), P(None, "boot"))
    out_specs = (P(None, "boot"), P(None, "tm"))
    return jax.shard_map(
        per_device, mesh=mesh, in_specs=in_specs, out_specs=out_specs, check_vma=False
    )
```

```python
import functools

import jax
import jax.numpy as jnp
from jax import lax
from jax.experimental import pallas as pl
from jax.experimental.pallas import tpu as pltpu
from jax.sharding import PartitionSpec as P

CHANNELS = 1024
LAGS = 4
FEAT = LAGS * CHANNELS
RESP = 32
NBLK = 6
CAP = 384
SEG = 512
ITERS = 3
CHEB = 5
HEAD = 16
WINDOW = 640
CHUNK = 128

RHO = 4.0
SHRINK = 0.75
EPSILON = 1e-05

HIGHEST = lax.Precision.HIGHEST
NT = (((1,), (1,)), ((), ()))
NN = (((1,), (0,)), ((), ()))
HALO, POWER, SUPPORT, SCATTER, GATHER, NORMS, BOOTS, FINAL = 0, 1, 2, 3, 6, 8, 9, 10
PHASES = 11


def split(a):
    high = a.astype(jnp.bfloat16)
    return high, (a - high.astype(jnp.float32)).astype(jnp.bfloat16)


def times(a, high, low):
    rows = a.shape[0]
    first, rest = split(a)
    out = jnp.dot(
        jnp.concatenate([first, rest], axis=0), high, preferred_element_type=jnp.float32
    )
    return out[:rows] + (out[rows:] + jnp.dot(first, low, preferred_element_type=jnp.float32))


def chebyshev(gram, rhs, bound):
    high, low = split(gram)
    theta = RHO + 0.5 * bound
    delta = 0.5 * bound
    sigma = theta / delta
    total = jnp.zeros_like(rhs)
    remain = rhs
    factor = 1.0 / sigma
    update = rhs / theta
    for count in range(CHEB):
        total = total + update
        if count + 1 < CHEB:
            applied = RHO * update + times(update, high, low)
            remain = remain - applied
            after = 1.0 / (2.0 * sigma - factor)
            update = after * factor * update + 2.0 * after / delta * remain
            factor = after
    return total


def chebyshev_terms(bound):
    theta = RHO + 0.5 * bound
    delta = 0.5 * bound
    sigma = theta / delta
    nought = jnp.zeros_like(bound)
    total = [nought] * CHEB
    remain = [jnp.ones_like(bound)] + [nought] * (CHEB - 1)
    factor = 1.0 / sigma
    update = [term / theta for term in remain]
    for count in range(CHEB):
        total = [a + b for a, b in zip(total, update)]
        if count + 1 < CHEB:
            applied = [
                theta * update[k] + (delta * update[k - 1] if k else 0.0)
                for k in range(CHEB)
            ]
            remain = [a - b for a, b in zip(remain, applied)]
            after = 1.0 / (2.0 * sigma - factor)
            update = [
                after * factor * d + 2.0 * after / delta * r
                for d, r in zip(update, remain)
            ]
            factor = after
    return total, delta


def far_first():
    offsets = [(d, p, a, c) for d in range(4) for p in range(2) for a in range(2) for c in range(2)]
    hops = {o: min(o[0], 4 - o[0]) + (2 if o[1] > o[2] else o[1] | o[2]) for o in offsets}
    return sorted(offsets[1:], key=lambda o: -hops[o])


def kernel(
    tm,
    boots,
    rec_hbm,
    starts_hbm,
    lengths_hbm,
    support_hbm,
    packed,
    rec,
    starts_ref,
    lengths_ref,
    halo,
    power,
    sup,
    ext,
    design,
    turned,
    cross,
    v,
    z,
    solver,
    solver_high,
    solver_low,
    outgoing,
    incoming,
    gathered,
    norms,
    zx,
    final,
    send_sem,
    recv_sem,
    local_sem,
):
    b = lax.axis_index("boot")
    me = lax.axis_index("tm")
    x, y, core = me // 8, lax.rem(me // 2, 4), lax.rem(me, 2)
    offsets = far_first()

    def tm_at(o):
        pair, place = lax.rem(y // 2 + o[1], 2), lax.rem(lax.rem(y, 2) + o[2], 2)
        return lax.rem(x + o[0], 4) * 8 + pair * 4 + place * 2 + lax.rem(core + o[3], 2)

    def tm_peer(i):
        return lax.rem(me + i, tm)

    def boot_peer(i):
        return lax.rem(b + i, boots)

    barrier = pltpu.get_barrier_semaphore()

    @pl.loop(1, tm)
    def _(i):
        pl.semaphore_signal(
            barrier, inc=1, device_id={"tm": tm_peer(i)}, device_id_type=pl.DeviceIdType.MESH
        )

    @pl.loop(1, boots)
    def _(i):
        pl.semaphore_signal(
            barrier, inc=1, device_id={"boot": boot_peer(i)}, device_id_type=pl.DeviceIdType.MESH
        )

    def fetch(src, dst, k):
        copy = pltpu.make_async_copy(src, dst, local_sem.at[k])
        copy.start()
        return copy

    rec_copy = fetch(rec_hbm, rec, 0)
    starts_copy = fetch(starts_hbm, starts_ref, 1)
    lengths_copy = fetch(lengths_hbm, lengths_ref, 2)
    support_copy = fetch(support_hbm, sup.at[b], 3)

    def send(src, dst, phase, target):
        pltpu.make_async_remote_copy(
            src_ref=src,
            dst_ref=dst,
            send_sem=send_sem.at[phase],
            recv_sem=recv_sem.at[phase],
            device_id=target,
            device_id_type=pl.DeviceIdType.MESH,
        ).start()

    def to_tm(src, dst, phase):
        for o in offsets:
            send(src, dst, phase, {"tm": tm_at(o)})

    def to_boots(src, dst, phase):
        for i in (4, 3, 5, 2, 6, 1, 7):
            send(src, dst, phase, {"boot": boot_peer(i)})

    def arrived(ref, phase):
        pltpu.make_async_copy(ref, ref, recv_sem.at[phase]).wait()

    def left(ref, phase):
        pltpu.make_async_copy(ref, ref, send_sem.at[phase]).wait()

    rec_copy.wait()
    acc = jnp.zeros((8, CHANNELS), jnp.float32)

    def add_rows(k, acc):
        block = rec[pl.ds(pl.multiple_of(k * 16, 16), 16), :].astype(jnp.float32)
        block = block * block
        return acc + block[:8] + block[8:]

    acc = lax.fori_loop(0, SEG // 16, add_rows, acc)
    power[me] = jnp.sum(acc, axis=0, keepdims=True)

    starts_copy.wait()
    lengths_copy.wait()
    row = lax.broadcasted_iota(jnp.int32, (CAP, CHUNK), 0)
    place = jnp.full((CAP, CHUNK), -4 * SEG, jnp.int32)
    offset = jnp.int32(0)
    for k in range(NBLK):
        length = lengths_ref[0, k]
        inside = (row >= offset) & (row < offset + length)
        place = jnp.where(inside, row + (starts_ref[0, k] - offset), place)
        offset = offset + length
    lane = lax.broadcasted_iota(jnp.int32, (CAP, CHUNK), 1)

    def picks(back, width):
        return jnp.concatenate(
            [
                jnp.where(place - back == lane + c * CHUNK, 1.0, 0.0).astype(jnp.bfloat16)
                for c in range(width // CHUNK)
            ],
            axis=1,
        )

    def raw_rows(lag):
        pick = picks(1 + lag, SEG)
        for part in range(4):
            at = lag * CHANNELS + part * 256
            design[:, at : at + 256] = jnp.dot(
                pick, rec[:, part * 256 : (part + 1) * 256], preferred_element_type=jnp.float32
            ).astype(jnp.bfloat16)

    support_copy.wait()
    raw_rows(0)
    pl.semaphore_wait(barrier, tm + boots - 2)
    send(rec_hbm.at[pl.ds(SEG - HEAD, HEAD)], halo, HALO, {"tm": tm_peer(1)})
    to_tm(power.at[me], power.at[me], POWER)
    to_boots(support_hbm, sup.at[b], SUPPORT)
    raw_rows(1)
    raw_rows(2)
    raw_rows(3)
    answer = jnp.dot(picks(0, SEG), rec[:, :CHUNK], preferred_element_type=jnp.float32)
    answer = jnp.transpose(answer)[:RESP]
    arrived(halo, HALO)
    before = halo[...]
    before = jnp.where(me == 0, jnp.zeros_like(before), before)
    behind = lane - HEAD
    for lag in range(LAGS):
        cols = slice(lag * CHANNELS, (lag + 1) * CHANNELS)
        reach = jnp.where(place - 1 - lag == behind, 1.0, 0.0).astype(jnp.bfloat16)[:, :HEAD]
        extra = jnp.dot(reach, before, preferred_element_type=jnp.float32)
        design[:, cols] = (design[:, cols].astype(jnp.float32) + extra).astype(jnp.bfloat16)
    arrived(power.at[pl.ds(0, tm - 1)], POWER)
    total = jnp.sum(power[...], axis=0)
    scale = 1.0 / jnp.sqrt(total / (SEG * tm) + EPSILON)

    diagonal = lax.broadcasted_iota(jnp.int32, (RESP, CHUNK), 0) == lane[:RESP]
    column = jnp.sum(jnp.where(diagonal, scale[:, :CHUNK], 0.0), axis=1, keepdims=True)
    answer = (answer * column).astype(jnp.bfloat16)
    both = jnp.zeros((CAP + RESP, CAP), jnp.float32)
    for lag in range(LAGS):
        cols = slice(lag * CHANNELS, (lag + 1) * CHANNELS)
        piece = (design[:, cols].astype(jnp.float32) * scale).astype(jnp.bfloat16)
        design[:, cols] = piece
        fit = jnp.dot(answer, piece, preferred_element_type=jnp.float32) * (1.0 / CAP)
        cross[:, cols] = fit
        both = both + lax.dot_general(
            jnp.concatenate([piece, fit.astype(jnp.bfloat16)], axis=0),
            piece,
            NT,
            preferred_element_type=jnp.float32,
        )
    gram = both[:CAP] * (1.0 / CAP)
    projected = both[CAP:]
    solver[...] = gram
    bound = jnp.sqrt(jnp.sum(jnp.sum(gram * gram, axis=1, keepdims=True), axis=0, keepdims=True))

    def flip(lag):
        cols = slice(lag * CHANNELS, (lag + 1) * CHANNELS)
        turned[cols, :] = jnp.transpose(design[:, cols])

    mine = pl.ds(pl.multiple_of(me * CHUNK, CHUNK), CHUNK)
    for it in range(ITERS):
        projected = projected * (1.0 / CAP)
        if it == 0:
            weights = chebyshev(solver[...], projected, bound)
        else:
            weights = times(projected, solver_high[...], solver_low[...])
        weights = weights.astype(jnp.bfloat16)
        if it:
            left(outgoing.at[pl.ds(0, tm - 1)], SCATTER + it - 1)
        for dx, dp in ((2, 1), (2, 0), (1, 1), (3, 1), (1, 0), (3, 0), (0, 1), (0, 0)):
            group = lax.rem(x + dx, 4) * 2 + lax.rem(y // 2 + dp, 2)
            cols = pl.ds(pl.multiple_of(group * 512, 512), 512)
            back = jnp.dot(weights, design[:, cols], preferred_element_type=jnp.float32)
            value = (cross[:, cols] - back) * (1.0 / RHO)
            v[:, cols] = value
            for c in range(4):
                outgoing[group * 4 + c] = value[:, c * CHUNK : (c + 1) * CHUNK].astype(jnp.bfloat16)
            for slot, o in enumerate(offsets):
                if o[:2] == (dx, dp):
                    peer = tm_at(o)
                    send(outgoing.at[peer], incoming.at[slot], SCATTER + it, {"tm": peer})

        if it == 0:
            terms, delta = chebyshev_terms(bound)
            ri = lax.broadcasted_iota(jnp.int32, (CAP, CAP), 0)
            ci = lax.broadcasted_iota(jnp.int32, (CAP, CAP), 1)
            eye = jnp.where(ri == ci, 1.0, 0.0)
            x1 = solver[...] * (1.0 / delta) - eye
            x2 = jnp.dot(x1, x1, precision=HIGHEST, preferred_element_type=jnp.float32)
            solver_high[...], solver_low[...] = split(
                terms[0] * eye
                + terms[1] * x1
                + terms[2] * x2
                + jnp.dot(
                    x2,
                    terms[3] * x1 + terms[4] * x2,
                    precision=HIGHEST,
                    preferred_element_type=jnp.float32,
                )
            )

            flip(0)

        arrived(incoming, SCATTER + it)
        mean = v[:, mine]
        for i in range(tm - 1):
            mean = mean + incoming[i].astype(jnp.float32)
        mean = mean * (1.0 / tm)
        if it:
            mean = mean + z[:, mine]
        if it + 1 < ITERS:
            if it:
                left(gathered.at[pl.ds(0, tm - 1)], GATHER + it - 1)
            gathered[me] = mean.astype(jnp.bfloat16)
            to_tm(gathered.at[me], gathered.at[me], GATHER + it)
            if it == 0:
                flip(1)
                flip(2)
                flip(3)
            else:
                def scale_rows(k, carry):
                    at = pl.multiple_of(k * 16, 16)
                    block = rec[pl.ds(at, 16), :].astype(jnp.float32) * scale
                    ext[pl.ds(pl.multiple_of(at + HEAD, 16), 16), :] = block.astype(jnp.bfloat16)
                    return carry

                lax.fori_loop(0, SEG // 16, scale_rows, 0)
                ext[0:HEAD, :] = (before.astype(jnp.float32) * scale).astype(jnp.bfloat16)
                ext[HEAD + SEG :, :] = jnp.zeros((WINDOW - HEAD - SEG, CHANNELS), jnp.bfloat16)
                normed = ext[HEAD : HEAD + SEG, :CHUNK].astype(jnp.float32)
                packed[:RESP] = jnp.transpose(normed)[:RESP]
            arrived(gathered.at[pl.ds(0, tm - 1)], GATHER + it)
            lengths = []
            for c in range(tm):
                block = gathered[c].astype(jnp.float32)
                lengths.append(jnp.sqrt(jnp.sum(block * block, axis=0, keepdims=True)))
            level = (
                jnp.sum(functools.reduce(jnp.add, lengths), axis=1, keepdims=True)
                * (SHRINK / FEAT)
            )
            projected = jnp.zeros((RESP, CAP), jnp.float32)
            for part in range(8):
                targets = []
                for c in range(part * 4, part * 4 + 4):
                    cols = slice(c * CHUNK, (c + 1) * CHUNK)
                    factor = jnp.maximum(lengths[c] - level, 0.0) / jnp.maximum(lengths[c], level)
                    fresh = gathered[c].astype(jnp.float32) * factor
                    dual = v[:, cols] - fresh
                    if it:
                        dual = dual + z[:, cols]
                    z[:, cols] = fresh
                    targets.append((cross[:, cols] + RHO * (fresh - dual)).astype(jnp.bfloat16))
                projected = projected + lax.dot_general(
                    jnp.concatenate(targets, axis=1),
                    turned[part * 512 : (part + 1) * 512, :],
                    NN,
                    preferred_element_type=jnp.float32,
                )
    length = jnp.sqrt(jnp.sum(mean * mean, axis=0, keepdims=True))
    norms[me] = length
    to_tm(norms.at[me], norms.at[me], NORMS)
    arrived(norms.at[pl.ds(0, tm - 1)], NORMS)
    level = jnp.sum(jnp.sum(norms[...], axis=0), axis=1, keepdims=True) * (SHRINK / FEAT)
    factor = jnp.maximum(length - level, 0.0) / jnp.maximum(length, level)
    zx[b] = (mean * factor).astype(jnp.bfloat16)
    to_boots(zx.at[b], zx.at[b], BOOTS)
    arrived(sup.at[pl.ds(0, boots - 1)], SUPPORT)
    quarter = pl.ds(pl.multiple_of(lax.rem(me, 4) * CHUNK, CHUNK), CHUNK)
    chosen = sup[me // 4, :, quarter].astype(jnp.float32)
    tally = jnp.maximum(jnp.sum(chosen, axis=0, keepdims=True), 1.0)
    arrived(zx.at[pl.ds(0, boots - 1)], BOOTS)
    average = jnp.zeros((RESP, CHUNK), jnp.float32)
    for k in range(boots):
        average = average + chosen[k : k + 1] * zx[k].astype(jnp.float32)
    average = average / tally
    final[me] = average.astype(jnp.bfloat16)
    to_tm(final.at[me], final.at[me], FINAL)
    arrived(final.at[pl.ds(0, tm - 1)], FINAL)
    for c in range(4):
        packed[2 * RESP :, c * CHUNK : (c + 1) * CHUNK] = final[4 * b + c].astype(jnp.float32)
    stacked = jnp.concatenate(
        [
            jnp.concatenate([final[lag * 8 + c] for c in range(8)], axis=1)
            for lag in range(LAGS)
        ],
        axis=0,
    )
    forecast = lax.dot_general(stacked, ext[...], NT, preferred_element_type=jnp.float32)
    told = jnp.zeros((RESP, SEG), jnp.float32)
    for lag in range(LAGS):
        begin = HEAD - 1 - lag
        shifted = pltpu.roll(forecast[lag * RESP : (lag + 1) * RESP], WINDOW - begin, 1)
        told = told + shifted[:, :SEG]
    packed[RESP : 2 * RESP] = told

    left(power.at[pl.ds(0, tm - 1)], POWER)
    left(halo, HALO)
    left(sup.at[pl.ds(0, boots - 1)], SUPPORT)
    left(outgoing.at[pl.ds(0, tm - 1)], SCATTER + ITERS - 1)
    left(gathered.at[pl.ds(0, tm - 1)], GATHER + ITERS - 2)
    left(norms.at[pl.ds(0, tm - 1)], NORMS)
    left(zx.at[pl.ds(0, boots - 1)], BOOTS)
    left(final.at[pl.ds(0, tm - 1)], FINAL)


def per_device(recording, starts, lengths, support):
    tm = lax.axis_size("tm")
    boots = lax.axis_size("boot")
    vmem = pl.BlockSpec(memory_space=pltpu.VMEM)
    anywhere = pl.BlockSpec(memory_space=pltpu.HBM)
    packed = pl.pallas_call(
        functools.partial(kernel, tm, boots),
        out_shape=jax.ShapeDtypeStruct((3 * RESP, SEG), jnp.float32),
        in_specs=[anywhere] * 4,
        out_specs=vmem,
        scratch_shapes=[
            pltpu.VMEM((SEG, CHANNELS), jnp.bfloat16),
            pltpu.SMEM((1, NBLK), jnp.int32),
            pltpu.SMEM((1, NBLK), jnp.int32),
            pltpu.VMEM((HEAD, CHANNELS), jnp.bfloat16),
            pltpu.VMEM((tm, 1, CHANNELS), jnp.float32),
            pltpu.VMEM((boots, boots, FEAT // boots), jnp.int32),
            pltpu.VMEM((WINDOW, CHANNELS), jnp.bfloat16),
            pltpu.VMEM((CAP, FEAT), jnp.bfloat16),
            pltpu.VMEM((FEAT, CAP), jnp.bfloat16),
            pltpu.VMEM((RESP, FEAT), jnp.float32),
            pltpu.VMEM((RESP, FEAT), jnp.float32),
            pltpu.VMEM((RESP, FEAT), jnp.float32),
            pltpu.VMEM((CAP, CAP), jnp.float32),
            pltpu.VMEM((CAP, CAP), jnp.bfloat16),
            pltpu.VMEM((CAP, CAP), jnp.bfloat16),
            pltpu.VMEM((tm, RESP, CHUNK), jnp.bfloat16),
            pltpu.VMEM((tm - 1, RESP, CHUNK), jnp.bfloat16),
            pltpu.VMEM((tm, RESP, CHUNK), jnp.bfloat16),
            pltpu.VMEM((tm, 1, CHUNK), jnp.float32),
            pltpu.VMEM((boots, RESP, CHUNK), jnp.bfloat16),
            pltpu.VMEM((tm, RESP, CHUNK), jnp.bfloat16),
            pltpu.SemaphoreType.DMA((PHASES,)),
            pltpu.SemaphoreType.DMA((PHASES,)),
            pltpu.SemaphoreType.DMA((4,)),
        ],
        compiler_params=pltpu.CompilerParams(
            collective_id=0, has_side_effects=True, vmem_limit_bytes=48 * 1024 * 1024
        ),
    )(*(pltpu.with_memory_space_constraint(a, pltpu.HBM) for a in (recording, starts, lengths, support)))
    return packed[2 * RESP :], packed[:RESP] - packed[RESP : 2 * RESP]


def solution(mesh):
    in_specs = (P("tm", None), P("boot", "tm"), P("boot", "tm"), P(None, "boot"))
    out_specs = (P(None, "boot"), P(None, "tm"))
    return jax.shard_map(
        per_device, mesh=mesh, in_specs=in_specs, out_specs=out_specs, check_vma=False
    )
```

```python
import functools

import jax
import jax.numpy as jnp
from jax import lax
from jax.experimental import pallas as pl
from jax.experimental.pallas import tpu as pltpu
from jax.sharding import PartitionSpec as P

CHANNELS = 1024
LAGS = 4
FEAT = LAGS * CHANNELS
RESP = 32
NBLK = 6
CAP = 384
SEG = 512
ITERS = 3
CHEB = 5
HEAD = 16
WINDOW = 640
CHUNK = 128

RHO = 4.0
SHRINK = 0.75
EPSILON = 1e-05

HIGHEST = lax.Precision.HIGHEST
NT = (((1,), (1,)), ((), ()))
NN = (((1,), (0,)), ((), ()))
HALO, POWER, SUPPORT, SCATTER, GATHER, NORMS, BOOTS, FINAL = 0, 1, 2, 3, 6, 8, 9, 10
PHASES = 11


def split(a):
    high = a.astype(jnp.bfloat16)
    return high, (a - high.astype(jnp.float32)).astype(jnp.bfloat16)


def times(a, high, low):
    rows = a.shape[0]
    first, rest = split(a)
    out = jnp.dot(
        jnp.concatenate([first, rest], axis=0), high, preferred_element_type=jnp.float32
    )
    return out[:rows] + (out[rows:] + jnp.dot(first, low, preferred_element_type=jnp.float32))


def chebyshev(gram, rhs, bound):
    high, low = split(gram)
    theta = RHO + 0.5 * bound
    delta = 0.5 * bound
    sigma = theta / delta
    total = jnp.zeros_like(rhs)
    remain = rhs
    factor = 1.0 / sigma
    update = rhs / theta
    for count in range(CHEB):
        total = total + update
        if count + 1 < CHEB:
            applied = RHO * update + times(update, high, low)
            remain = remain - applied
            after = 1.0 / (2.0 * sigma - factor)
            update = after * factor * update + 2.0 * after / delta * remain
            factor = after
    return total


def chebyshev_terms(bound):
    theta = RHO + 0.5 * bound
    delta = 0.5 * bound
    sigma = theta / delta
    nought = jnp.zeros_like(bound)
    total = [nought] * CHEB
    remain = [jnp.ones_like(bound)] + [nought] * (CHEB - 1)
    factor = 1.0 / sigma
    update = [term / theta for term in remain]
    for count in range(CHEB):
        total = [a + b for a, b in zip(total, update)]
        if count + 1 < CHEB:
            applied = [
                theta * update[k] + (delta * update[k - 1] if k else 0.0)
                for k in range(CHEB)
            ]
            remain = [a - b for a, b in zip(remain, applied)]
            after = 1.0 / (2.0 * sigma - factor)
            update = [
                after * factor * d + 2.0 * after / delta * r
                for d, r in zip(update, remain)
            ]
            factor = after
    return total, delta


def far_first():
    offsets = [(d, p, a, c) for d in range(4) for p in range(2) for a in range(2) for c in range(2)]
    hops = {o: min(o[0], 4 - o[0]) + (2 if o[1] > o[2] else o[1] | o[2]) for o in offsets}
    return sorted(offsets[1:], key=lambda o: -hops[o])


def kernel(
    tm,
    boots,
    rec_hbm,
    starts_hbm,
    lengths_hbm,
    support_hbm,
    packed,
    rec,
    starts_ref,
    lengths_ref,
    halo,
    power,
    sup,
    ext,
    design,
    turned,
    cross,
    v,
    z,
    solver,
    solver_high,
    solver_low,
    outgoing,
    incoming,
    gathered,
    norms,
    zx,
    final,
    send_sem,
    recv_sem,
    local_sem,
):
    b = lax.axis_index("boot")
    me = lax.axis_index("tm")
    x, y, core = me // 8, lax.rem(me // 2, 4), lax.rem(me, 2)
    offsets = far_first()

    def tm_at(o):
        pair, place = lax.rem(y // 2 + o[1], 2), lax.rem(lax.rem(y, 2) + o[2], 2)
        return lax.rem(x + o[0], 4) * 8 + pair * 4 + place * 2 + lax.rem(core + o[3], 2)

    def tm_peer(i):
        return lax.rem(me + i, tm)

    def boot_peer(i):
        return lax.rem(b + i, boots)

    barrier = pltpu.get_barrier_semaphore()

    for o in offsets:
        pl.semaphore_signal(
            barrier, inc=1, device_id={"tm": tm_at(o)}, device_id_type=pl.DeviceIdType.MESH
        )

    @pl.loop(1, boots)
    def _(i):
        pl.semaphore_signal(
            barrier, inc=1, device_id={"boot": boot_peer(i)}, device_id_type=pl.DeviceIdType.MESH
        )

    def fetch(src, dst, k):
        copy = pltpu.make_async_copy(src, dst, local_sem.at[k])
        copy.start()
        return copy

    rec_copy = fetch(rec_hbm, rec, 0)
    starts_copy = fetch(starts_hbm, starts_ref, 1)
    lengths_copy = fetch(lengths_hbm, lengths_ref, 2)
    support_copy = fetch(support_hbm, sup.at[b], 3)

    def send(src, dst, phase, target):
        pltpu.make_async_remote_copy(
            src_ref=src,
            dst_ref=dst,
            send_sem=send_sem.at[phase],
            recv_sem=recv_sem.at[phase],
            device_id=target,
            device_id_type=pl.DeviceIdType.MESH,
        ).start()

    def to_tm(src, dst, phase):
        for o in offsets:
            send(src, dst, phase, {"tm": tm_at(o)})

    def to_boots(src, dst, phase):
        for i in (4, 3, 5, 2, 6, 1, 7):
            send(src, dst, phase, {"boot": boot_peer(i)})

    def arrived(ref, phase):
        pltpu.make_async_copy(ref, ref, recv_sem.at[phase]).wait()

    def left(ref, phase):
        pltpu.make_async_copy(ref, ref, send_sem.at[phase]).wait()

    rec_copy.wait()
    acc = jnp.zeros((8, CHANNELS), jnp.float32)

    def add_rows(k, acc):
        block = rec[pl.ds(pl.multiple_of(k * 16, 16), 16), :].astype(jnp.float32)
        block = block * block
        return acc + block[:8] + block[8:]

    acc = lax.fori_loop(0, SEG // 16, add_rows, acc)
    power[me] = jnp.sum(acc, axis=0, keepdims=True)

    starts_copy.wait()
    lengths_copy.wait()
    row = lax.broadcasted_iota(jnp.int32, (CAP, CHUNK), 0)
    place = jnp.full((CAP, CHUNK), -4 * SEG, jnp.int32)
    offset = jnp.int32(0)
    for k in range(NBLK):
        length = lengths_ref[0, k]
        inside = (row >= offset) & (row < offset + length)
        place = jnp.where(inside, row + (starts_ref[0, k] - offset), place)
        offset = offset + length
    lane = lax.broadcasted_iota(jnp.int32, (CAP, CHUNK), 1)

    def picks(back, width):
        return jnp.concatenate(
            [
                jnp.where(place - back == lane + c * CHUNK, 1.0, 0.0).astype(jnp.bfloat16)
                for c in range(width // CHUNK)
            ],
            axis=1,
        )

    def raw_rows(lag):
        pick = picks(1 + lag, SEG)
        for part in range(4):
            at = lag * CHANNELS + part * 256
            design[:, at : at + 256] = jnp.dot(
                pick, rec[:, part * 256 : (part + 1) * 256], preferred_element_type=jnp.float32
            ).astype(jnp.bfloat16)

    support_copy.wait()
    raw_rows(0)
    pl.semaphore_wait(barrier, tm + boots - 2)
    send(rec_hbm.at[pl.ds(SEG - HEAD, HEAD)], halo, HALO, {"tm": tm_peer(1)})
    to_tm(power.at[me], power.at[me], POWER)
    to_boots(support_hbm, sup.at[b], SUPPORT)
    raw_rows(1)
    raw_rows(2)
    raw_rows(3)
    answer = jnp.dot(picks(0, SEG), rec[:, :CHUNK], preferred_element_type=jnp.float32)
    answer = jnp.transpose(answer)[:RESP]
    arrived(halo, HALO)
    before = halo[...]
    before = jnp.where(me == 0, jnp.zeros_like(before), before)
    behind = lane - HEAD
    for lag in range(LAGS):
        cols = slice(lag * CHANNELS, (lag + 1) * CHANNELS)
        reach = jnp.where(place - 1 - lag == behind, 1.0, 0.0).astype(jnp.bfloat16)[:, :HEAD]
        extra = jnp.dot(reach, before, preferred_element_type=jnp.float32)
        design[:, cols] = (design[:, cols].astype(jnp.float32) + extra).astype(jnp.bfloat16)
    arrived(power.at[pl.ds(0, tm - 1)], POWER)
    total = jnp.sum(power[...], axis=0)
    scale = 1.0 / jnp.sqrt(total / (SEG * tm) + EPSILON)

    diagonal = lax.broadcasted_iota(jnp.int32, (RESP, CHUNK), 0) == lane[:RESP]
    column = jnp.sum(jnp.where(diagonal, scale[:, :CHUNK], 0.0), axis=1, keepdims=True)
    answer = (answer * column).astype(jnp.bfloat16)
    both = jnp.zeros((CAP + RESP, CAP), jnp.float32)
    for lag in range(LAGS):
        cols = slice(lag * CHANNELS, (lag + 1) * CHANNELS)
        piece = (design[:, cols].astype(jnp.float32) * scale).astype(jnp.bfloat16)
        design[:, cols] = piece
        fit = jnp.dot(answer, piece, preferred_element_type=jnp.float32) * (1.0 / CAP)
        cross[:, cols] = fit
        both = both + lax.dot_general(
            jnp.concatenate([piece, fit.astype(jnp.bfloat16)], axis=0),
            piece,
            NT,
            preferred_element_type=jnp.float32,
        )
    gram = both[:CAP] * (1.0 / CAP)
    projected = both[CAP:]
    solver[...] = gram
    bound = jnp.sqrt(jnp.sum(jnp.sum(gram * gram, axis=1, keepdims=True), axis=0, keepdims=True))

    def flip(lag):
        cols = slice(lag * CHANNELS, (lag + 1) * CHANNELS)
        turned[cols, :] = jnp.transpose(design[:, cols])

    mine = pl.ds(pl.multiple_of(me * CHUNK, CHUNK), CHUNK)
    for it in range(ITERS):
        projected = projected * (1.0 / CAP)
        if it == 0:
            weights = chebyshev(solver[...], projected, bound)
        else:
            weights = times(projected, solver_high[...], solver_low[...])
        weights = weights.astype(jnp.bfloat16)
        if it:
            left(outgoing.at[pl.ds(0, tm - 1)], SCATTER + it - 1)
        for dx, dp in ((2, 1), (2, 0), (1, 1), (3, 1), (1, 0), (3, 0), (0, 1), (0, 0)):
            group = lax.rem(x + dx, 4) * 2 + lax.rem(y // 2 + dp, 2)
            cols = pl.ds(pl.multiple_of(group * 512, 512), 512)
            back = jnp.dot(weights, design[:, cols], preferred_element_type=jnp.float32)
            value = (cross[:, cols] - back) * (1.0 / RHO)
            v[:, cols] = value
            for c in range(4):
                outgoing[group * 4 + c] = value[:, c * CHUNK : (c + 1) * CHUNK].astype(jnp.bfloat16)
            for slot, o in enumerate(offsets):
                if o[:2] == (dx, dp):
                    peer = tm_at(o)
                    send(outgoing.at[peer], incoming.at[slot], SCATTER + it, {"tm": peer})

        if it == 0:
            terms, delta = chebyshev_terms(bound)
            ri = lax.broadcasted_iota(jnp.int32, (CAP, CAP), 0)
            ci = lax.broadcasted_iota(jnp.int32, (CAP, CAP), 1)
            eye = jnp.where(ri == ci, 1.0, 0.0)
            x1 = solver[...] * (1.0 / delta) - eye
            x2 = jnp.dot(x1, x1, precision=HIGHEST, preferred_element_type=jnp.float32)
            solver_high[...], solver_low[...] = split(
                terms[0] * eye
                + terms[1] * x1
                + terms[2] * x2
                + jnp.dot(
                    x2,
                    terms[3] * x1 + terms[4] * x2,
                    precision=HIGHEST,
                    preferred_element_type=jnp.float32,
                )
            )

            flip(0)

        arrived(incoming, SCATTER + it)
        mean = v[:, mine]
        for i in range(tm - 1):
            mean = mean + incoming[i].astype(jnp.float32)
        mean = mean * (1.0 / tm)
        if it:
            mean = mean + z[:, mine]
        if it + 1 < ITERS:
            if it:
                left(gathered.at[pl.ds(0, tm - 1)], GATHER + it - 1)
            gathered[me] = mean.astype(jnp.bfloat16)
            to_tm(gathered.at[me], gathered.at[me], GATHER + it)
            if it == 0:
                flip(1)
                flip(2)
                flip(3)
            else:
                def scale_rows(k, carry):
                    at = pl.multiple_of(k * 16, 16)
                    block = rec[pl.ds(at, 16), :].astype(jnp.float32) * scale
                    ext[pl.ds(pl.multiple_of(at + HEAD, 16), 16), :] = block.astype(jnp.bfloat16)
                    return carry

                lax.fori_loop(0, SEG // 16, scale_rows, 0)
                ext[0:HEAD, :] = (before.astype(jnp.float32) * scale).astype(jnp.bfloat16)
                ext[HEAD + SEG :, :] = jnp.zeros((WINDOW - HEAD - SEG, CHANNELS), jnp.bfloat16)
                normed = ext[HEAD : HEAD + SEG, :CHUNK].astype(jnp.float32)
                packed[:RESP] = jnp.transpose(normed)[:RESP]
            arrived(gathered.at[pl.ds(0, tm - 1)], GATHER + it)
            lengths = []
            for c in range(tm):
                block = gathered[c].astype(jnp.float32)
                lengths.append(jnp.sqrt(jnp.sum(block * block, axis=0, keepdims=True)))
            level = (
                jnp.sum(functools.reduce(jnp.add, lengths), axis=1, keepdims=True)
                * (SHRINK / FEAT)
            )
            projected = jnp.zeros((RESP, CAP), jnp.float32)
            for part in range(8):
                targets = []
                for c in range(part * 4, part * 4 + 4):
                    cols = slice(c * CHUNK, (c + 1) * CHUNK)
                    factor = jnp.maximum(lengths[c] - level, 0.0) / jnp.maximum(lengths[c], level)
                    fresh = gathered[c].astype(jnp.float32) * factor
                    dual = v[:, cols] - fresh
                    if it:
                        dual = dual + z[:, cols]
                    z[:, cols] = fresh
                    targets.append((cross[:, cols] + RHO * (fresh - dual)).astype(jnp.bfloat16))
                projected = projected + lax.dot_general(
                    jnp.concatenate(targets, axis=1),
                    turned[part * 512 : (part + 1) * 512, :],
                    NN,
                    preferred_element_type=jnp.float32,
                )
    length = jnp.sqrt(jnp.sum(mean * mean, axis=0, keepdims=True))
    norms[me] = length
    to_tm(norms.at[me], norms.at[me], NORMS)
    arrived(norms.at[pl.ds(0, tm - 1)], NORMS)
    level = jnp.sum(jnp.sum(norms[...], axis=0), axis=1, keepdims=True) * (SHRINK / FEAT)
    factor = jnp.maximum(length - level, 0.0) / jnp.maximum(length, level)
    zx[b] = (mean * factor).astype(jnp.bfloat16)
    to_boots(zx.at[b], zx.at[b], BOOTS)
    arrived(sup.at[pl.ds(0, boots - 1)], SUPPORT)
    quarter = pl.ds(pl.multiple_of(lax.rem(me, 4) * CHUNK, CHUNK), CHUNK)
    chosen = sup[me // 4, :, quarter].astype(jnp.float32)
    tally = jnp.maximum(jnp.sum(chosen, axis=0, keepdims=True), 1.0)
    arrived(zx.at[pl.ds(0, boots - 1)], BOOTS)
    average = jnp.zeros((RESP, CHUNK), jnp.float32)
    for k in range(boots):
        average = average + chosen[k : k + 1] * zx[k].astype(jnp.float32)
    average = average / tally
    final[me] = average.astype(jnp.bfloat16)
    to_tm(final.at[me], final.at[me], FINAL)
    arrived(final.at[pl.ds(0, tm - 1)], FINAL)
    for c in range(4):
        packed[2 * RESP :, c * CHUNK : (c + 1) * CHUNK] = final[4 * b + c].astype(jnp.float32)
    stacked = jnp.concatenate(
        [
            jnp.concatenate([final[lag * 8 + c] for c in range(8)], axis=1)
            for lag in range(LAGS)
        ],
        axis=0,
    )
    forecast = lax.dot_general(stacked, ext[...], NT, preferred_element_type=jnp.float32)
    told = jnp.zeros((RESP, SEG), jnp.float32)
    for lag in range(LAGS):
        begin = HEAD - 1 - lag
        shifted = pltpu.roll(forecast[lag * RESP : (lag + 1) * RESP], WINDOW - begin, 1)
        told = told + shifted[:, :SEG]
    packed[RESP : 2 * RESP] = told

    left(power.at[pl.ds(0, tm - 1)], POWER)
    left(halo, HALO)
    left(sup.at[pl.ds(0, boots - 1)], SUPPORT)
    left(outgoing.at[pl.ds(0, tm - 1)], SCATTER + ITERS - 1)
    left(gathered.at[pl.ds(0, tm - 1)], GATHER + ITERS - 2)
    left(norms.at[pl.ds(0, tm - 1)], NORMS)
    left(zx.at[pl.ds(0, boots - 1)], BOOTS)
    left(final.at[pl.ds(0, tm - 1)], FINAL)


def per_device(recording, starts, lengths, support):
    tm = lax.axis_size("tm")
    boots = lax.axis_size("boot")
    vmem = pl.BlockSpec(memory_space=pltpu.VMEM)
    anywhere = pl.BlockSpec(memory_space=pltpu.HBM)
    packed = pl.pallas_call(
        functools.partial(kernel, tm, boots),
        out_shape=jax.ShapeDtypeStruct((3 * RESP, SEG), jnp.float32),
        in_specs=[anywhere] * 4,
        out_specs=vmem,
        scratch_shapes=[
            pltpu.VMEM((SEG, CHANNELS), jnp.bfloat16),
            pltpu.SMEM((1, NBLK), jnp.int32),
            pltpu.SMEM((1, NBLK), jnp.int32),
            pltpu.VMEM((HEAD, CHANNELS), jnp.bfloat16),
            pltpu.VMEM((tm, 1, CHANNELS), jnp.float32),
            pltpu.VMEM((boots, boots, FEAT // boots), jnp.int32),
            pltpu.VMEM((WINDOW, CHANNELS), jnp.bfloat16),
            pltpu.VMEM((CAP, FEAT), jnp.bfloat16),
            pltpu.VMEM((FEAT, CAP), jnp.bfloat16),
            pltpu.VMEM((RESP, FEAT), jnp.float32),
            pltpu.VMEM((RESP, FEAT), jnp.float32),
            pltpu.VMEM((RESP, FEAT), jnp.float32),
            pltpu.VMEM((CAP, CAP), jnp.float32),
            pltpu.VMEM((CAP, CAP), jnp.bfloat16),
            pltpu.VMEM((CAP, CAP), jnp.bfloat16),
            pltpu.VMEM((tm, RESP, CHUNK), jnp.bfloat16),
            pltpu.VMEM((tm - 1, RESP, CHUNK), jnp.bfloat16),
            pltpu.VMEM((tm, RESP, CHUNK), jnp.bfloat16),
            pltpu.VMEM((tm, 1, CHUNK), jnp.float32),
            pltpu.VMEM((boots, RESP, CHUNK), jnp.bfloat16),
            pltpu.VMEM((tm, RESP, CHUNK), jnp.bfloat16),
            pltpu.SemaphoreType.DMA((PHASES,)),
            pltpu.SemaphoreType.DMA((PHASES,)),
            pltpu.SemaphoreType.DMA((4,)),
        ],
        compiler_params=pltpu.CompilerParams(
            collective_id=0, has_side_effects=True, vmem_limit_bytes=48 * 1024 * 1024
        ),
    )(*(pltpu.with_memory_space_constraint(a, pltpu.HBM) for a in (recording, starts, lengths, support)))
    return packed[2 * RESP :], packed[:RESP] - packed[RESP : 2 * RESP]


def solution(mesh):
    in_specs = (P("tm", None), P("boot", "tm"), P("boot", "tm"), P(None, "boot"))
    out_specs = (P(None, "boot"), P(None, "tm"))
    return jax.shard_map(
        per_device, mesh=mesh, in_specs=in_specs, out_specs=out_specs, check_vma=False
    )
```
